256 devices in a mesh: seq: 32 (over z, x_lo, core), chan: 8 (over x_hi, y).
Axes of the slice: x: 4 (x_hi: 2, x_lo: 2; x = x_hi * 2 + x_lo), y: 4, z: 8, core: 2. Of those that a mesh axis runs over, the one named last changes fastest.
Arguments:
- query_rows: bfloat16 [16384, 4096], P('seq', 'chan'), may hold values from -6 to 6
- key_rows: bfloat16 [16384, 4096], P('seq', 'chan'), may hold values from -6 to 6
- value_rows: bfloat16 [16384, 4096], P('seq', 'chan'), may hold values from -6 to 6
- filter_taps: float32 [16384, 4096], P('seq', 'chan'), may hold values from -1 to 1
- skip_gain: float32 [4096], P('chan'), may hold values from 0.5 to 1.5
- w_out: bfloat16 [4096, 8192], P('chan'), may hold values from -0.09375 to 0.09375
Outputs:
- mixed: bfloat16 [16384, 8192], P('seq', 'chan')
The draws below stay inside these ranges and needn't reach their ends.
All inputs are finite; a program needn't handle non-finite values.
Results may differ from the reference program's by a relative error of at most 0.005.
Values may be sent and summed in bfloat16 or wider, within the bound.
A program may use at most 192 MiB of HBM per device.

```python
import math
import jax
import jax.numpy as jnp
from jax import lax

DM = 8192
CH = 4096
TOKENS = 16384


def shared_rows(key):
    return jax.random.truncated_normal(key, -4.0, 4.0, (TOKENS, CH), jnp.float32)


def draw_key_rows(key, part):
    common = shared_rows(key)
    key = jax.random.fold_in(key, 5)
    own_rows = jax.random.truncated_normal(key, -4.0, 4.0, (TOKENS, CH), jnp.float32)
    return (0.8 * common + 0.6 * own_rows).astype(jnp.bfloat16)


def draw_value_rows(key, part):
    common = shared_rows(key)
    key = jax.random.fold_in(key, 7)
    own_rows = jax.random.truncated_normal(key, -4.0, 4.0, (TOKENS, CH), jnp.float32)
    return (0.8 * common + 0.6 * own_rows).astype(jnp.bfloat16)


def draw_filter_taps(key, part):
    key = jax.random.fold_in(key, 11)
    key_pick, key_slow, key_fast, key_noise = jax.random.split(key, 4)
    slow_share = 0.5
    noise_taps = jax.random.truncated_normal(key_noise, -2.3, 2.3, (TOKENS, CH), jnp.float32)
    chosen = jax.random.uniform(key_pick, (CH,), jnp.float32) < slow_share
    slow_rate = jnp.exp(jax.random.uniform(key_slow, (CH,), jnp.float32, math.log(0.2 / TOKENS), math.log(2.0 / TOKENS)))
    fast_rate = jnp.exp(jax.random.uniform(key_fast, (CH,), jnp.float32, math.log(1.0 / 50.0), math.log(1.0 / 10.0)))
    rates = jnp.where(chosen, slow_rate, fast_rate)
    scaling = jnp.sqrt((1.0 - jnp.exp(-2.0 * rates)) / (1.0 - jnp.exp(-2.0 * rates * TOKENS)))
    steps_pos = jnp.arange(TOKENS, dtype=jnp.float32)[:, None]
    return noise_taps * jnp.exp(-rates * steps_pos) * scaling + 1.0 / TOKENS


def steps_of(rng, dims, cuts, low, top_value):
    gain = 1.0
    for position, blocks in cuts:
        heights = jax.random.uniform(jax.random.fold_in(jax.random.fold_in(rng, 6), position), (blocks,), jnp.float32, low / len(cuts), top_value / len(cuts))
        gain = gain * jnp.repeat(jnp.exp(heights), dims[position] // blocks).reshape((-1,) + (1,) * (len(dims) - 1 - position))
    return gain


def centred(own_key, shape, deviation, most, cuts=(), kind=jnp.bfloat16):
    level = steps_of(own_key, shape, cuts, -0.22, 0.18) if cuts else 1.0
    values = jax.random.normal(own_key, shape, jnp.float32) * deviation * level
    return jnp.minimum(jnp.maximum(values, -most), most).astype(kind)


def setup_inputs(seed: int = 0) -> dict:
    seeds = jax.random.split(jax.random.key(seed), 7)
    query_rows = centred(seeds[0], (TOKENS, CH), 1.0, 6.0, ((0, 32), (1, 8)))
    key_rows = draw_key_rows(jax.random.fold_in(seeds[6], 71), 0)
    value_rows = draw_value_rows(jax.random.fold_in(seeds[6], 71), 0)
    filter_taps = draw_filter_taps(jax.random.fold_in(seeds[6], 71), 0)
    skip_gain = jnp.clip(0.5 + 1.0 * jax.random.uniform(seeds[4], (CH,), jnp.float32) ** steps_of(seeds[4], (CH,), ((0, 8),), -0.2, 0.2), 0.5, 1.5)
    w_out = centred(seeds[5], (CH, DM), CH ** -0.5, 0.09375, ((0, 8),))
    return {"query_rows": query_rows, "key_rows": key_rows, "value_rows": value_rows, "filter_taps": filter_taps, "skip_gain": skip_gain, "w_out": w_out}


def convolve(operands):
    signal, taps = operands
    padded_len = 2 * signal.shape[0]
    spectrum = jnp.fft.rfft(signal, n=padded_len, axis=0) * jnp.fft.rfft(taps, n=padded_len, axis=0)
    return jnp.fft.irfft(spectrum, n=padded_len, axis=0)[: signal.shape[0]]


def reference(query_rows, key_rows, value_rows, filter_taps, skip_gain, w_out):
    product = key_rows.astype(jnp.float32) * value_rows.astype(jnp.float32)
    width_block = 128 if CH % 128 == 0 else CH
    block_count = CH // width_block
    signal_blocks = product.reshape(TOKENS, block_count, width_block).transpose(1, 0, 2)
    taps_blocks = filter_taps.reshape(TOKENS, block_count, width_block).transpose(1, 0, 2)
    convolved = lax.map(convolve, (signal_blocks, taps_blocks))
    convolved = convolved.transpose(1, 0, 2).reshape(TOKENS, CH).astype(jnp.float32)
    gated = (query_rows.astype(jnp.float32) * (convolved + skip_gain * product)).astype(jnp.bfloat16)
    return jnp.dot(gated, w_out, preferred_element_type=jnp.float32).astype(jnp.bfloat16)
```

```python
import functools

import jax
import jax.numpy as jnp
import ml_dtypes
import numpy as np
from jax import lax
from jax.experimental import pallas as pl
from jax.experimental.pallas import tpu as pltpu
from jax.sharding import PartitionSpec as P

MESH = pl.DeviceIdType.MESH
LANES = 128
CHUNKS = 2
BF16 = jnp.bfloat16
F32 = jnp.float32


def split_table(table):
    high = table.astype(ml_dtypes.bfloat16)
    low = (table - high.astype(np.float64)).astype(ml_dtypes.bfloat16)
    return high, low


def transform_tables(seq_count, row_groups):
    coarse = seq_count * row_groups
    total = coarse * LANES
    freq = np.arange(coarse) + 0.25
    order = (np.arange(seq_count)[None, :] * row_groups + np.arange(row_groups)[:, None]).reshape(-1)
    angle = 2.0 * np.pi * freq[:, None] * order[None, :] / coarse
    forward_first = np.concatenate((np.cos(angle), -np.sin(angle)), axis=0)
    inverse_first = np.concatenate((np.cos(angle).T, -np.sin(angle).T), axis=1) / total
    fine = np.arange(LANES)
    turn = 2.0 * np.pi * freq[:, None] * fine[None, :] / total
    twist_cos = np.cos(turn).astype(np.float32)
    twist_sin = np.sin(turn).astype(np.float32)
    inner = 2.0 * np.pi * (fine[:, None] * fine[None, :] % LANES) / LANES
    cosine, sine = np.cos(inner), np.sin(inner)
    forward_second = np.block([[cosine, -sine], [sine, cosine]])
    inverse_second = np.block([[cosine, sine], [-sine, cosine]])
    return (
        np.concatenate(split_table(forward_first), axis=1),
        twist_cos,
        twist_sin,
        *split_table(forward_second),
        *split_table(inverse_second),
        *split_table(inverse_first),
    )


def mm(left, right):
    return jnp.dot(left, right, preferred_element_type=F32)


def mm_nt(left, right):
    return lax.dot_general(left, right, (((1,), (1,)), ((), ())), preferred_element_type=F32)


def split(value):
    high = value.astype(BF16)
    low = (value - high.astype(F32)).astype(BF16)
    return high, low


def eye(size):
    row = lax.broadcasted_iota(jnp.int32, (size, size), 0)
    col = lax.broadcasted_iota(jnp.int32, (size, size), 1)
    return (row == col).astype(F32).astype(BF16)


def kernel(
    seq_count, chan_count,
    q_ref, k_ref, v_ref, h_ref, skip_ref, w_ref,
    first_ref, tcos_ref, tsin_ref, sec_hi, sec_lo, isec_hi, isec_lo, ifirst_hi, ifirst_lo,
    out_ref,
    send, recv, staged, ysend, yrecv, ybuf, gown, gall, wall, acc,
    send_sem, recv_sem, ysend_sem, yrecv_sem, gsend_sem, grecv_sem,
    wsend_sem, wrecv_sem, fsend_sem, frecv_sem, wown_sem,
):
    rows, channels = q_ref.shape
    groups = rows // LANES
    width = channels // CHUNKS
    per = width // seq_count
    coarse = seq_count * groups
    cols = out_ref.shape[1]
    half_rows = channels // 2
    y_count = chan_count // 2
    me = lax.axis_index("seq")
    chan = lax.axis_index("chan")
    core = me % 2
    flipped = me + 2 - 4 * ((me // 2) % 2)
    x_hi = chan // y_count
    sibling = me + 1 - 2 * core

    def w_peer(j):
        other = (chan + j) % chan_count
        seq_to = jnp.where(other // y_count == x_hi, me, flipped)
        return other, seq_to

    barrier = pltpu.get_barrier_semaphore()

    @pl.loop(1, seq_count)
    def _(j):
        pl.semaphore_signal(barrier, inc=1, device_id={"seq": (me + j) % seq_count, "chan": chan}, device_id_type=MESH)

    @pl.loop(1, chan_count)
    def _(j):
        pl.semaphore_signal(barrier, inc=1, device_id={"seq": me, "chan": (chan + j) % chan_count}, device_id_type=MESH)

    @pl.loop(0, y_count)
    def _(j):
        other = ((1 - x_hi) * y_count) + j
        pl.semaphore_signal(barrier, inc=1, device_id={"seq": flipped, "chan": other}, device_id_type=MESH)

    def prepare(n):
        cut = slice(n * width, (n + 1) * width)
        unit = eye(width)
        product = (k_ref[:, cut].astype(F32) * v_ref[:, cut].astype(F32)).astype(BF16)
        p_rows = mm_nt(unit, product).reshape(seq_count, per, rows)
        h_rows = mm_nt(unit, h_ref[:, cut].astype(BF16)).reshape(seq_count, per, rows)
        send[n] = jnp.concatenate((p_rows, h_rows), axis=1).astype(BF16)

    prepare(0)
    pl.semaphore_wait(barrier, seq_count - 1 + chan_count - 1 + y_count)

    def block_copy(n, slot_out, slot_in, to):
        return pltpu.make_async_remote_copy(
            src_ref=send.at[n, slot_out], dst_ref=recv.at[n, slot_in],
            send_sem=send_sem.at[n, slot_out], recv_sem=recv_sem.at[n, slot_in],
            device_id={"seq": to, "chan": chan}, device_id_type=MESH)

    def back_copy(n, slot_out, slot_in, to):
        return pltpu.make_async_remote_copy(
            src_ref=ysend.at[n, slot_out], dst_ref=yrecv.at[n, slot_in],
            send_sem=ysend_sem.at[n, slot_out], recv_sem=yrecv_sem.at[n, slot_in],
            device_id={"seq": to, "chan": chan}, device_id_type=MESH)

    def gated_copy(n, slot_in, other):
        return pltpu.make_async_remote_copy(
            src_ref=gown.at[n], dst_ref=gall.at[n, slot_in],
            send_sem=gsend_sem.at[n, other], recv_sem=grecv_sem.at[n, slot_in],
            device_id={"seq": me, "chan": other}, device_id_type=MESH)

    own_half = pl.ds(pl.multiple_of(core * half_rows, half_rows), half_rows)

    def w_copy(slot_in, other, seq_to):
        return pltpu.make_async_remote_copy(
            src_ref=w_ref.at[own_half, pl.ds(pl.multiple_of(other * cols, cols), cols)],
            dst_ref=wall.at[slot_in, own_half],
            send_sem=wsend_sem.at[other], recv_sem=wrecv_sem.at[slot_in],
            device_id={"seq": seq_to, "chan": other}, device_id_type=MESH)

    def w_share(slot, half):
        part = pl.ds(pl.multiple_of(half * half_rows, half_rows), half_rows)
        return pltpu.make_async_remote_copy(
            src_ref=wall.at[slot, part], dst_ref=wall.at[slot, part],
            send_sem=fsend_sem.at[slot], recv_sem=frecv_sem.at[slot],
            device_id={"seq": sibling, "chan": chan}, device_id_type=MESH)

    w_own = pltpu.make_async_copy(w_ref.at[:, pl.ds(pl.multiple_of(chan * cols, cols), cols)], wall.at[chan], wown_sem)

    def start_blocks(n):
        @pl.loop(1, seq_count)
        def _(j):
            to = (me + j) % seq_count
            block_copy(n, to, me, to).start()
        recv[n, me] = send[n, me]

    def convolve(n):
        @pl.loop(1, seq_count)
        def _(j):
            source = (me + j) % seq_count
            block_copy(n, source, source, source).wait_recv()

        for g in range(groups):
            staged[g] = recv[n, :, :, g * LANES:(g + 1) * LANES].astype(F32).reshape(seq_count * 2 * per, LANES)

        def gather_rows(row):
            parts = [staged[g, pl.ds(row, seq_count, stride=2 * per)] for g in range(groups)]
            return jnp.concatenate(parts, axis=0)

        def spectrum(row):
            signal = jnp.concatenate((gather_rows(row), gather_rows(row + per)), axis=1).astype(BF16)
            stage = mm(first_ref[...], jnp.concatenate((signal, signal), axis=0))
            cosine = jnp.concatenate((tcos_ref[...], tcos_ref[...]), axis=1)
            sine = jnp.concatenate((tsin_ref[...], tsin_ref[...]), axis=1)
            real, imag = stage[:coarse], stage[coarse:]
            turned_re = real * cosine + imag * sine
            turned_im = imag * cosine - real * sine
            joined = jnp.concatenate((
                jnp.concatenate((turned_re[:, :LANES], turned_im[:, :LANES]), axis=1),
                jnp.concatenate((turned_re[:, LANES:], turned_im[:, LANES:]), axis=1)), axis=0)
            high, low = split(joined)
            both = mm(high, sec_hi[...]) + mm(low, sec_hi[...]) + mm(high, sec_lo[...])
            p_re, p_im = both[:coarse, :LANES], both[:coarse, LANES:]
            h_re, h_im = both[coarse:, :LANES], both[coarse:, LANES:]
            return jnp.concatenate((p_re * h_re - p_im * h_im, p_re * h_im + p_im * h_re), axis=1)

        def pair(step):
            first = 2 * step
            spectra = jnp.concatenate((spectrum(first), spectrum(first + 1)), axis=0)
            high, low = split(spectra)
            back = mm(high, isec_hi[...]) + mm(low, isec_hi[...]) + mm(high, isec_lo[...])
            cosine = jnp.concatenate((tcos_ref[...], tcos_ref[...]), axis=0)
            sine = jnp.concatenate((tsin_ref[...], tsin_ref[...]), axis=0)
            real, imag = back[:, :LANES], back[:, LANES:]
            turned_re = real * cosine - imag * sine
            turned_im = imag * cosine + real * sine
            joined = jnp.concatenate((
                jnp.concatenate((turned_re[:coarse], turned_re[coarse:]), axis=1),
                jnp.concatenate((turned_im[:coarse], turned_im[coarse:]), axis=1)), axis=0)
            high, low = split(joined)
            result = mm(ifirst_hi[...], high) + mm(ifirst_hi[...], low) + mm(ifirst_lo[...], high)
            for c in range(2):
                for g in range(groups):
                    ybuf[g % 2, pl.ds((g // 2) * per + first + c, seq_count, stride=2 * per)] = (
                        result[g * seq_count:(g + 1) * seq_count, c * LANES:(c + 1) * LANES])

        @pl.loop(0, per // 2)
        def _(step):
            pair(step)

        for g in range(2):
            ysend[n, :, :, g * LANES:(g + 1) * LANES] = ybuf[g].astype(BF16).reshape(seq_count, 2 * per, LANES)

        @pl.loop(1, seq_count)
        def _(j):
            to = (me + j) % seq_count
            back_copy(n, to, me, to).start()
        yrecv[n, me] = ysend[n, me]

    def gate(n):
        @pl.loop(1, seq_count)
        def _(j):
            source = (me + j) % seq_count
            back_copy(n, source, source, source).wait_recv()

        cut = slice(n * width, (n + 1) * width)
        unit = eye(rows // 2)
        arrived = yrecv[n].astype(F32).reshape(seq_count, 2, per, rows // 2)
        for part in range(2):
            at = slice(part * (rows // 2), (part + 1) * (rows // 2))
            conv = mm_nt(unit, arrived[:, part].reshape(width, rows // 2).astype(BF16))
            product = k_ref[at, cut].astype(F32) * v_ref[at, cut].astype(F32)
            gated = q_ref[at, cut].astype(F32) * (conv + skip_ref[:, cut] * product)
            gown[n, at] = gated.astype(BF16)

        @pl.loop(1, chan_count)
        def _(j):
            gated_copy(n, chan, (chan + j) % chan_count).start()

    def project(n):
        for j in range(chan_count):
            source = (chan + j) % chan_count
            if j > 0:
                gated_copy(n, source, source).wait_recv()
                left = gall[n, source]
            else:
                left = gown[n]
            term = mm(left, wall[source, n * width:(n + 1) * width])
            if n == 0 and j == 0:
                acc[...] = term
            elif n == CHUNKS - 1 and j == chan_count - 1:
                out_ref[...] = (acc[...] + term).astype(BF16)
            else:
                acc[...] += term

    start_blocks(0)
    prepare(1)
    start_blocks(1)
    w_own.start()

    @pl.loop(1, chan_count)
    def _(j):
        other, seq_to = w_peer(j)
        w_copy(chan, other, seq_to).start()

    convolve(0)
    convolve(1)
    gate(0)

    @pl.loop(1, chan_count)
    def _(j):
        other, seq_to = w_peer(j)
        w_copy(other, other, seq_to).wait_recv()
        w_share(other, core).start()

    gate(1)
    w_own.wait()

    @pl.loop(1, chan_count)
    def _(j):
        other, seq_to = w_peer(j)
        w_share(other, 1 - core).wait_recv()

    project(0)
    project(1)

    @pl.loop(1, seq_count)
    def _(j):
        to = (me + j) % seq_count
        for n in range(CHUNKS):
            block_copy(n, to, to, to).wait_send()
            back_copy(n, to, to, to).wait_send()

    @pl.loop(1, chan_count)
    def _(j):
        other, seq_to = w_peer(j)
        for n in range(CHUNKS):
            gated_copy(n, other, other).wait_send()
        w_copy(other, other, seq_to).wait_send()
        w_share(other, core).wait_send()


def on_device(seq_count, chan_count, query_rows, key_rows, value_rows, filter_taps, skip_gain, w_out):
    rows, channels = query_rows.shape
    cols = w_out.shape[1] // chan_count
    width = channels // CHUNKS
    per = width // seq_count
    tables = [jnp.asarray(t) for t in transform_tables(seq_count, rows // LANES)]
    vmem = pl.BlockSpec(memory_space=pltpu.VMEM)
    dma = pltpu.SemaphoreType.DMA
    return pl.pallas_call(
        functools.partial(kernel, seq_count, chan_count),
        out_shape=jax.ShapeDtypeStruct((rows, cols), BF16),
        in_specs=[vmem] * 5 + [pl.BlockSpec(memory_space=pl.ANY)] + [vmem] * len(tables),
        out_specs=vmem,
        scratch_shapes=[
            pltpu.VMEM((CHUNKS, seq_count, 2 * per, rows), BF16),
            pltpu.VMEM((CHUNKS, seq_count, 2 * per, rows), BF16),
            pltpu.VMEM((rows // LANES, seq_count * 2 * per, LANES), F32),
            pltpu.VMEM((CHUNKS, seq_count, 2 * per, rows // 2), BF16),
            pltpu.VMEM((CHUNKS, seq_count, 2 * per, rows // 2), BF16),
            pltpu.VMEM((2, seq_count * 2 * per, LANES), F32),
            pltpu.VMEM((CHUNKS, rows, width), BF16),
            pltpu.VMEM((CHUNKS, chan_count, rows, width), BF16),
            pltpu.VMEM((chan_count, channels, cols), BF16),
            pltpu.VMEM((rows, cols), F32),
            dma((CHUNKS, seq_count)), dma((CHUNKS, seq_count)),
            dma((CHUNKS, seq_count)), dma((CHUNKS, seq_count)),
            dma((CHUNKS, chan_count)), dma((CHUNKS, chan_count)),
            dma((chan_count,)), dma((chan_count,)), dma((chan_count,)), dma((chan_count,)),
            dma,
        ],
        compiler_params=pltpu.CompilerParams(
            collective_id=0, has_side_effects=True, vmem_limit_bytes=56 * 1024 * 1024),
    )(query_rows, key_rows, value_rows, filter_taps, skip_gain.reshape(1, channels), w_out, *tables)


def solution(mesh):
    return jax.shard_map(
        functools.partial(on_device, mesh.shape["seq"], mesh.shape["chan"]),
        mesh=mesh,
        in_specs=(
            P("seq", "chan"),
            P("seq", "chan"),
            P("seq", "chan"),
            P("seq", "chan"),
            P("chan"),
            P("chan", None),
        ),
        out_specs=P("seq", "chan"),
        check_vma=False,
    )
```

```python
import functools

import jax
import jax.numpy as jnp
import ml_dtypes
import numpy as np
from jax import lax
from jax.experimental import pallas as pl
from jax.experimental.pallas import tpu as pltpu
from jax.sharding import PartitionSpec as P

MESH = pl.DeviceIdType.MESH
LANES = 128
CHUNKS = 2
BF16 = jnp.bfloat16
F32 = jnp.float32


def split_table(table):
    high = table.astype(ml_dtypes.bfloat16)
    low = (table - high.astype(np.float64)).astype(ml_dtypes.bfloat16)
    return high, low


def transform_tables(seq_count, row_groups):
    coarse = seq_count * row_groups
    total = coarse * LANES
    freq = np.arange(coarse) + 0.25
    order = (np.arange(seq_count)[None, :] * row_groups + np.arange(row_groups)[:, None]).reshape(-1)
    angle = 2.0 * np.pi * freq[:, None] * order[None, :] / coarse
    forward_first = np.concatenate((np.cos(angle), -np.sin(angle)), axis=0)
    inverse_first = np.concatenate((np.cos(angle).T, -np.sin(angle).T), axis=1) / total
    fine = np.arange(LANES)
    turn = 2.0 * np.pi * freq[:, None] * fine[None, :] / total
    twist_cos = np.cos(turn).astype(np.float32)
    twist_sin = np.sin(turn).astype(np.float32)
    inner = 2.0 * np.pi * (fine[:, None] * fine[None, :] % LANES) / LANES
    cosine, sine = np.cos(inner), np.sin(inner)
    forward_second = np.block([[cosine, -sine], [sine, cosine]])
    inverse_second = np.block([[cosine, sine], [-sine, cosine]])
    return (
        np.concatenate(split_table(forward_first), axis=1),
        twist_cos,
        twist_sin,
        *split_table(forward_second),
        *split_table(inverse_second),
        *split_table(inverse_first),
    )


def mm(left, right):
    return jnp.dot(left, right, preferred_element_type=F32)


def mm_nt(left, right):
    return lax.dot_general(left, right, (((1,), (1,)), ((), ())), preferred_element_type=F32)


def split(value):
    high = value.astype(BF16)
    low = (value - high.astype(F32)).astype(BF16)
    return high, low


def eye(size):
    row = lax.broadcasted_iota(jnp.int32, (size, size), 0)
    col = lax.broadcasted_iota(jnp.int32, (size, size), 1)
    return (row == col).astype(F32).astype(BF16)


def kernel(
    seq_count, chan_count,
    q_ref, k_ref, v_ref, h_ref, skip_ref, w_ref,
    first_ref, tcos_ref, tsin_ref, sec_hi, sec_lo, isec_hi, isec_lo, ifirst_hi, ifirst_lo,
    out_ref,
    send, recv, staged, ysend, yrecv, ybuf, gall, wall, acc, psend, precv,
    send_sem, recv_sem, ysend_sem, yrecv_sem, gsend_sem, grecv_sem, psend_sem, precv_sem,
    wsend_sem, wrecv_sem, fsend_sem, frecv_sem, wown_sem,
):
    rows, channels = q_ref.shape
    groups = rows // LANES
    width = channels // CHUNKS
    per = width // seq_count
    coarse = seq_count * groups
    cols = out_ref.shape[1]
    y_count = chan_count // 2
    half = rows // 2
    me = lax.axis_index("seq")
    chan = lax.axis_index("chan")
    core = me % 2
    x_lo = (me // 2) % 2
    parity = (me // 4) % 2
    sibling = me + 1 - 2 * core
    mate = me + 2 - 4 * x_lo
    above = (me + 4) % seq_count
    below = (me + seq_count - 4) % seq_count
    x_hi = chan // y_count
    y = chan % y_count
    facing = (1 - x_hi) * y_count + y

    def y_peer(j):
        return (y + j) % y_count

    def device(seq_to, chan_to):
        return {"seq": seq_to, "chan": chan_to}

    barrier = pltpu.get_barrier_semaphore()

    @pl.loop(1, seq_count)
    def _(j):
        pl.semaphore_signal(barrier, inc=1, device_id=device((me + j) % seq_count, chan), device_id_type=MESH)

    @pl.loop(1, y_count)
    def _(j):
        pl.semaphore_signal(barrier, inc=1, device_id=device(me, x_hi * y_count + y_peer(j)), device_id_type=MESH)

    pl.semaphore_signal(barrier, inc=1, device_id=device(me, facing), device_id_type=MESH)

    def prepare(n):
        cut = slice(n * width, (n + 1) * width)
        unit = eye(width)
        product = (k_ref[:, cut].astype(F32) * v_ref[:, cut].astype(F32)).astype(BF16)
        p_rows = mm_nt(unit, product).reshape(seq_count, per, rows)
        h_rows = mm_nt(unit, h_ref[:, cut].astype(BF16)).reshape(seq_count, per, rows)
        send[n] = jnp.concatenate((p_rows, h_rows), axis=1).astype(BF16)

    prepare(0)
    pl.semaphore_wait(barrier, seq_count + y_count - 1)

    def block_copy(n, slot_out, slot_in, to):
        return pltpu.make_async_remote_copy(
            src_ref=send.at[n, slot_out], dst_ref=recv.at[n, slot_in],
            send_sem=send_sem.at[n, slot_out], recv_sem=recv_sem.at[n, slot_in],
            device_id={"seq": to, "chan": chan}, device_id_type=MESH)

    def back_copy(n, slot_out, slot_in, to):
        return pltpu.make_async_remote_copy(
            src_ref=ysend.at[n, slot_out], dst_ref=yrecv.at[n, slot_in],
            send_sem=ysend_sem.at[n, slot_out], recv_sem=yrecv_sem.at[n, slot_in],
            device_id={"seq": to, "chan": chan}, device_id_type=MESH)

    def gated_copy(n, part, slot, to):
        lanes = pl.ds(pl.multiple_of(slot * width, width), width)
        block = gall.at[n, pl.ds(part * half, half), lanes]
        return pltpu.make_async_remote_copy(
            src_ref=block, dst_ref=block,
            send_sem=gsend_sem.at[n, part, to], recv_sem=grecv_sem.at[n, part, slot],
            device_id=device(me, x_hi * y_count + to), device_id_type=MESH)

    def partial_copy(part):
        at = pl.ds(part * half, half)
        return pltpu.make_async_remote_copy(
            src_ref=psend.at[at], dst_ref=precv.at[at],
            send_sem=psend_sem.at[part], recv_sem=precv_sem.at[part],
            device_id=device(me, facing), device_id_type=MESH)

    core_rows = width // 2
    direct, by_pair, by_level = width // 8, width // 16, width // 8
    pair_base = direct
    level_base = direct + 2 * by_pair
    classes = (
        (direct, lambda: core * core_rows),
        (by_pair, lambda: core * core_rows + pair_base + x_lo * by_pair),
        (by_level, lambda: core * core_rows + level_base + parity * by_level),
    )

    def some_rows(start, size):
        return pl.ds(pl.multiple_of(start, 16), size)

    def side_of(col_side, x_side, y_side):
        target = jnp.where(col_side == 0, x_side, 1 - x_side)
        return pl.ds(pl.multiple_of((target * y_count + y_side) * cols, cols), cols)

    def w_copy(kind, col_side, slot, to):
        size, start = classes[kind]
        return pltpu.make_async_remote_copy(
            src_ref=w_ref.at[:, some_rows(start(), size), side_of(col_side, x_hi, to)],
            dst_ref=wall.at[:, slot, some_rows(start(), size), pl.ds(col_side * cols, cols)],
            send_sem=wsend_sem.at[kind, col_side, to], recv_sem=wrecv_sem.at[kind, col_side, slot],
            device_id=device(me, x_hi * y_count + to), device_id_type=MESH)

    def w_pass(route, slot, start, size, seq_to):
        block = wall.at[:, slot, some_rows(start, size)]
        return pltpu.make_async_remote_copy(
            src_ref=block, dst_ref=block,
            send_sem=fsend_sem.at[route, slot], recv_sem=frecv_sem.at[route, slot],
            device_id=device(seq_to, chan), device_id_type=MESH)

    def pass_pair(slot, x_side):
        return w_pass(0, slot, core * core_rows + pair_base + x_side * by_pair, by_pair, mate)

    def pass_level(up, slot, level_side):
        size = by_level // 2
        start = core * core_rows + level_base + level_side * by_level + (0 if up else size)
        return w_pass(1 if up else 2, slot, start, size, above if up else below)

    def pass_core(slot, side):
        return w_pass(3, slot, side * core_rows, core_rows, sibling)

    def own_copy(col_side):
        return pltpu.make_async_copy(
            w_ref.at[:, :, side_of(col_side, x_hi, y)],
            wall.at[:, y, :, pl.ds(col_side * cols, cols)], wown_sem.at[col_side])

    def start_w(kind):
        @pl.loop(1, y_count)
        def _(j):
            for col_side in range(2):
                w_copy(kind, col_side, y, y_peer(j)).start()

    def wait_w(kind):
        @pl.loop(1, y_count)
        def _(j):
            for col_side in range(2):
                w_copy(kind, col_side, y_peer(j), y_peer(j)).wait_recv()

    def share_w():
        wait_w(1)

        @pl.loop(1, y_count)
        def _(j):
            pass_pair(y_peer(j), x_lo).start()

        wait_w(2)

        @pl.loop(1, y_count)
        def _(j):
            pass_level(True, y_peer(j), parity).start()
            pass_level(False, y_peer(j), parity).start()

    def finish_w():
        wait_w(0)

        @pl.loop(1, y_count)
        def _(j):
            slot = y_peer(j)
            pass_pair(slot, 1 - x_lo).wait_recv()
            pass_level(True, slot, 1 - parity).wait_recv()
            pass_level(False, slot, 1 - parity).wait_recv()
            pass_core(slot, core).start()

        own_copy(0).wait()
        own_copy(1).wait()

        @pl.loop(1, y_count)
        def _(j):
            pass_core(y_peer(j), 1 - core).wait_recv()

    def start_blocks(n):
        @pl.loop(1, seq_count)
        def _(j):
            to = (me + j) % seq_count
            block_copy(n, to, me, to).start()
        recv[n, me] = send[n, me]

    def convolve(n):
        @pl.loop(1, seq_count)
        def _(j):
            source = (me + j) % seq_count
            block_copy(n, source, source, source).wait_recv()

        for g in range(groups):
            staged[g] = recv[n, :, :, g * LANES:(g + 1) * LANES].astype(F32).reshape(seq_count * 2 * per, LANES)

        def gather_rows(row):
            parts = [staged[g, pl.ds(row, seq_count, stride=2 * per)] for g in range(groups)]
            return jnp.concatenate(parts, axis=0)

        def spectrum(row):
            signal = jnp.concatenate((gather_rows(row), gather_rows(row + per)), axis=1).astype(BF16)
            stage = mm(first_ref[...], jnp.concatenate((signal, signal), axis=0))
            cosine = jnp.concatenate((tcos_ref[...], tcos_ref[...]), axis=1)
            sine = jnp.concatenate((tsin_ref[...], tsin_ref[...]), axis=1)
            real, imag = stage[:coarse], stage[coarse:]
            turned_re = real * cosine + imag * sine
            turned_im = imag * cosine - real * sine
            joined = jnp.concatenate((
                jnp.concatenate((turned_re[:, :LANES], turned_im[:, :LANES]), axis=1),
                jnp.concatenate((turned_re[:, LANES:], turned_im[:, LANES:]), axis=1)), axis=0)
            high, low = split(joined)
            both = mm(high, sec_hi[...]) + mm(low, sec_hi[...]) + mm(high, sec_lo[...])
            p_re, p_im = both[:coarse, :LANES], both[:coarse, LANES:]
            h_re, h_im = both[coarse:, :LANES], both[coarse:, LANES:]
            return jnp.concatenate((p_re * h_re - p_im * h_im, p_re * h_im + p_im * h_re), axis=1)

        def pair(step):
            first = 2 * step
            spectra = jnp.concatenate((spectrum(first), spectrum(first + 1)), axis=0)
            high, low = split(spectra)
            back = mm(high, isec_hi[...]) + mm(low, isec_hi[...]) + mm(high, isec_lo[...])
            cosine = jnp.concatenate((tcos_ref[...], tcos_ref[...]), axis=0)
            sine = jnp.concatenate((tsin_ref[...], tsin_ref[...]), axis=0)
            real, imag = back[:, :LANES], back[:, LANES:]
            turned_re = real * cosine - imag * sine
            turned_im = imag * cosine + real * sine
            joined = jnp.concatenate((
                jnp.concatenate((turned_re[:coarse], turned_re[coarse:]), axis=1),
                jnp.concatenate((turned_im[:coarse], turned_im[coarse:]), axis=1)), axis=0)
            high, low = split(joined)
            result = mm(ifirst_hi[...], high) + mm(ifirst_hi[...], low) + mm(ifirst_lo[...], high)
            for c in range(2):
                for g in range(groups):
                    ybuf[g % 2, pl.ds((g // 2) * per + first + c, seq_count, stride=2 * per)] = (
                        result[g * seq_count:(g + 1) * seq_count, c * LANES:(c + 1) * LANES])

        @pl.loop(0, per // 2)
        def _(step):
            pair(step)

        for g in range(2):
            ysend[n, :, :, g * LANES:(g + 1) * LANES] = ybuf[g].astype(BF16).reshape(seq_count, 2 * per, LANES)

        @pl.loop(1, seq_count)
        def _(j):
            to = (me + j) % seq_count
            back_copy(n, to, me, to).start()
        yrecv[n, me] = ysend[n, me]

    def gate(n):
        @pl.loop(1, seq_count)
        def _(j):
            source = (me + j) % seq_count
            back_copy(n, source, source, source).wait_recv()

        cut = slice(n * width, (n + 1) * width)
        unit = eye(half)
        arrived = yrecv[n].astype(F32).reshape(seq_count, 2, per, half)
        lanes = pl.ds(pl.multiple_of(y * width, width), width)
        for part in range(2):
            at = slice(part * half, (part + 1) * half)
            conv = mm_nt(unit, arrived[:, part].reshape(width, half).astype(BF16))
            product = k_ref[at, cut].astype(F32) * v_ref[at, cut].astype(F32)
            gated = q_ref[at, cut].astype(F32) * (conv + skip_ref[:, cut] * product)
            gall[n, at, lanes] = gated.astype(BF16)

        @pl.loop(1, y_count)
        def _(j):
            for part in range(2):
                gated_copy(n, part, y, y_peer(j)).start()

    def wait_gated(n, part):
        @pl.loop(1, y_count)
        def _(j):
            gated_copy(n, part, y_peer(j), y_peer(j)).wait_recv()

    tile = min(cols, 512)
    tiles = cols // tile

    def term(n, part, lanes):
        at = slice(part * half, (part + 1) * half)
        return mm(gall[n, at], wall[n, :, :, lanes].reshape(y_count * width, tile))

    def tile_at(side, step):
        return pl.ds(pl.multiple_of(side * cols + step * tile, tile), tile)

    def project_first():
        for part in range(2):
            wait_gated(0, part)

            @pl.loop(0, 2 * tiles)
            def _(step):
                acc[part * half:(part + 1) * half, tile_at(0, step)] = term(0, part, tile_at(0, step))

    def project_last():
        for part in range(2):
            at = slice(part * half, (part + 1) * half)
            wait_gated(1, part)

            @pl.loop(0, tiles)
            def _(step):
                psend[at, tile_at(0, step)] = (acc[at, tile_at(1, step)] + term(1, part, tile_at(1, step))).astype(BF16)

            partial_copy(part).start()

        for part in range(2):
            at = slice(part * half, (part + 1) * half)

            @pl.loop(0, tiles)
            def _(step):
                acc[at, tile_at(0, step)] += term(1, part, tile_at(0, step))

        for part in range(2):
            at = slice(part * half, (part + 1) * half)
            partial_copy(part).wait_recv()
            out_ref[at] = (acc[at, :cols] + precv[at].astype(F32)).astype(BF16)

    start_blocks(0)
    prepare(1)
    start_blocks(1)
    start_w(2)
    start_w(1)
    start_w(0)
    own_copy(0).start()
    own_copy(1).start()
    convolve(0)
    convolve(1)
    share_w()
    gate(0)
    gate(1)
    finish_w()
    project_first()
    project_last()

    @pl.loop(1, seq_count)
    def _(j):
        to = (me + j) % seq_count
        for n in range(CHUNKS):
            block_copy(n, to, to, to).wait_send()
            back_copy(n, to, to, to).wait_send()

    @pl.loop(1, y_count)
    def _(j):
        slot = y_peer(j)
        for n in range(CHUNKS):
            for part in range(2):
                gated_copy(n, part, y, slot).wait_send()
        for kind in range(3):
            for col_side in range(2):
                w_copy(kind, col_side, y, slot).wait_send()
        pass_pair(slot, x_lo).wait_send()
        pass_level(True, slot, parity).wait_send()
        pass_level(False, slot, parity).wait_send()
        pass_core(slot, core).wait_send()

    for part in range(2):
        partial_copy(part).wait_send()


def on_device(seq_count, chan_count, query_rows, key_rows, value_rows, filter_taps, skip_gain, w_out):
    rows, channels = query_rows.shape
    cols = w_out.shape[1] // chan_count
    width = channels // CHUNKS
    per = width // seq_count
    y_count = chan_count // 2
    tables = [jnp.asarray(t) for t in transform_tables(seq_count, rows // LANES)]
    vmem = pl.BlockSpec(memory_space=pltpu.VMEM)
    dma = pltpu.SemaphoreType.DMA
    return pl.pallas_call(
        functools.partial(kernel, seq_count, chan_count),
        out_shape=jax.ShapeDtypeStruct((rows, cols), BF16),
        in_specs=[vmem] * 5 + [pl.BlockSpec(memory_space=pl.ANY)] + [vmem] * len(tables),
        out_specs=vmem,
        scratch_shapes=[
            pltpu.VMEM((CHUNKS, seq_count, 2 * per, rows), BF16),
            pltpu.VMEM((CHUNKS, seq_count, 2 * per, rows), BF16),
            pltpu.VMEM((rows // LANES, seq_count * 2 * per, LANES), F32),
            pltpu.VMEM((CHUNKS, seq_count, 2 * per, rows // 2), BF16),
            pltpu.VMEM((CHUNKS, seq_count, 2 * per, rows // 2), BF16),
            pltpu.VMEM((2, seq_count * 2 * per, LANES), F32),
            pltpu.VMEM((CHUNKS, rows, y_count * width), BF16),
            pltpu.VMEM((CHUNKS, y_count, width, 2 * cols), BF16),
            pltpu.VMEM((rows, 2 * cols), F32),
            pltpu.VMEM((rows, cols), BF16),
            pltpu.VMEM((rows, cols), BF16),
            dma((CHUNKS, seq_count)), dma((CHUNKS, seq_count)),
            dma((CHUNKS, seq_count)), dma((CHUNKS, seq_count)),
            dma((CHUNKS, 2, y_count)), dma((CHUNKS, 2, y_count)),
            dma((2,)), dma((2,)),
            dma((3, 2, y_count)), dma((3, 2, y_count)),
            dma((4, y_count)), dma((4, y_count)),
            dma((2,)),
        ],
        compiler_params=pltpu.CompilerParams(
            collective_id=0, has_side_effects=True, vmem_limit_bytes=56 * 1024 * 1024),
    )(query_rows, key_rows, value_rows, filter_taps, skip_gain.reshape(1, channels),
      w_out.reshape(CHUNKS, width, w_out.shape[1]), *tables)


def solution(mesh):
    return jax.shard_map(
        functools.partial(on_device, mesh.shape["seq"], mesh.shape["chan"]),
        mesh=mesh,
        in_specs=(
            P("seq", "chan"),
            P("seq", "chan"),
            P("seq", "chan"),
            P("seq", "chan"),
            P("chan"),
            P("chan", None),
        ),
        out_specs=P("seq", "chan"),
        check_vma=False,
    )
```

```python
import functools

import jax
import jax.numpy as jnp
import ml_dtypes
import numpy as np
from jax import lax
from jax.experimental import pallas as pl
from jax.experimental.pallas import tpu as pltpu
from jax.sharding import PartitionSpec as P

MESH = pl.DeviceIdType.MESH
LANES = 128
CHUNKS = 2
PARTS = 4
BF16 = jnp.bfloat16
F32 = jnp.float32


def split_table(table):
    high = table.astype(ml_dtypes.bfloat16)
    low = (table - high.astype(np.float64)).astype(ml_dtypes.bfloat16)
    return high, low


def transform_tables(seq_count, row_groups):
    coarse = seq_count * row_groups
    total = coarse * LANES
    freq = np.arange(coarse) + 0.25
    order = (np.arange(seq_count)[None, :] * row_groups + np.arange(row_groups)[:, None]).reshape(-1)
    angle = 2.0 * np.pi * freq[:, None] * order[None, :] / coarse
    forward_first = np.concatenate((np.cos(angle), -np.sin(angle)), axis=0)
    inverse_first = np.concatenate((np.cos(angle).T, -np.sin(angle).T), axis=1) / total
    fine = np.arange(LANES)
    turn = 2.0 * np.pi * freq[:, None] * fine[None, :] / total
    twist_cos = np.cos(turn).astype(np.float32)
    twist_sin = np.sin(turn).astype(np.float32)
    inner = 2.0 * np.pi * (fine[:, None] * fine[None, :] % LANES) / LANES
    cosine, sine = np.cos(inner), np.sin(inner)
    forward_second = np.block([[cosine, -sine], [sine, cosine]])
    inverse_second = np.block([[cosine, sine], [-sine, cosine]])
    turns = np.stack((twist_cos, twist_sin))
    inner = np.stack((*split_table(forward_second), *split_table(inverse_second)))
    first = np.concatenate(split_table(forward_first), axis=1)
    last = np.stack(split_table(inverse_first))
    return turns, inner, first, last


def mm(left, right):
    return jnp.dot(left, right, preferred_element_type=F32)


def mm_nt(left, right):
    return lax.dot_general(left, right, (((1,), (1,)), ((), ())), preferred_element_type=F32)


def split(value):
    high = value.astype(BF16)
    low = (value - high.astype(F32)).astype(BF16)
    return high, low


def eye(size):
    row = lax.broadcasted_iota(jnp.int32, (size, size), 0)
    col = lax.broadcasted_iota(jnp.int32, (size, size), 1)
    return (row == col).astype(F32).astype(BF16)


def kernel(
    seq_count, chan_count,
    q_hbm, k_hbm, v_hbm, h_hbm, skip_hbm, w_ref, turns_hbm, inner_hbm, first_hbm, last_hbm,
    own_ref, precv,
    q_ref, k_ref, v_ref, h_ref, skip_ref, turns_ref, inner_ref, first_ref, last_ref, load_sem,
    send, recv, staged, ysend, yrecv, ybuf, gall, wall, acc, psend,
    send_sem, recv_sem, ysend_sem, yrecv_sem, gsend_sem, grecv_sem, psend_sem, precv_sem,
    wsend_sem, wrecv_sem, fsend_sem, frecv_sem, wown_sem, own_sem,
):
    rows, channels = q_ref.shape
    groups = rows // LANES
    width = channels // CHUNKS
    per = width // seq_count
    coarse = seq_count * groups
    cols = own_ref.shape[1]
    y_count = chan_count // 2
    half = rows // 2
    part_rows = rows // PARTS
    me = lax.axis_index("seq")
    chan = lax.axis_index("chan")
    core = me % 2
    x_lo = (me // 2) % 2
    sibling = me + 1 - 2 * core
    mate = me + 2 - 4 * x_lo
    x_hi = chan // y_count
    y = chan % y_count
    facing = (1 - x_hi) * y_count + y

    def y_peer(j):
        return (y + j) % y_count

    def device(seq_to, chan_to):
        return {"seq": seq_to, "chan": chan_to}

    barrier = pltpu.get_barrier_semaphore()

    @pl.loop(1, seq_count)
    def _(j):
        pl.semaphore_signal(barrier, inc=1, device_id=device((me + j) % seq_count, chan), device_id_type=MESH)

    @pl.loop(1, y_count)
    def _(j):
        pl.semaphore_signal(barrier, inc=1, device_id=device(me, x_hi * y_count + y_peer(j)), device_id_type=MESH)

    pl.semaphore_signal(barrier, inc=1, device_id=device(me, facing), device_id_type=MESH)

    loads = [pltpu.make_async_copy(source, target, load_sem.at[i]) for i, (source, target) in enumerate((
        (k_hbm, k_ref), (v_hbm, v_ref), (h_hbm, h_ref), (turns_hbm, turns_ref), (inner_hbm, inner_ref),
        (first_hbm, first_ref), (last_hbm, last_ref), (q_hbm, q_ref), (skip_hbm, skip_ref)))]
    for load in loads:
        load.start()
    for load in loads[:3]:
        load.wait()

    def prepare(n):
        cut = slice(n * width, (n + 1) * width)
        unit = eye(width)
        product = (k_ref[:, cut].astype(F32) * v_ref[:, cut].astype(F32)).astype(BF16)
        p_rows = mm_nt(unit, product).reshape(seq_count, per, rows)
        h_rows = mm_nt(unit, h_ref[:, cut].astype(BF16)).reshape(seq_count, per, rows)
        send[n] = jnp.concatenate((p_rows, h_rows), axis=1).astype(BF16)

    prepare(0)
    pl.semaphore_wait(barrier, seq_count + y_count - 1)

    def block_copy(n, slot_out, slot_in, to):
        return pltpu.make_async_remote_copy(
            src_ref=send.at[n, slot_out], dst_ref=recv.at[n, slot_in],
            send_sem=send_sem.at[n], recv_sem=recv_sem.at[n],
            device_id={"seq": to, "chan": chan}, device_id_type=MESH)

    def back_copy(n, slot_out, slot_in, to):
        return pltpu.make_async_remote_copy(
            src_ref=ysend.at[n, slot_out], dst_ref=yrecv.at[n, slot_in],
            send_sem=ysend_sem.at[n], recv_sem=yrecv_sem.at[n],
            device_id={"seq": to, "chan": chan}, device_id_type=MESH)

    def gated_copy(n, part, lanes, to):
        block = gall.at[n, pl.ds(part * part_rows, part_rows), lanes]
        return pltpu.make_async_remote_copy(
            src_ref=block, dst_ref=block,
            send_sem=gsend_sem.at[n, part], recv_sem=grecv_sem.at[n, part],
            device_id=device(me, x_hi * y_count + to), device_id_type=MESH)

    def all_gated(n, part):
        return gated_copy(n, part, pl.ds(0, (y_count - 1) * width), y)

    def partial_copy(part):
        at = pl.ds(part * part_rows, part_rows)
        return pltpu.make_async_remote_copy(
            src_ref=psend.at[at], dst_ref=precv.at[at],
            send_sem=psend_sem.at[part], recv_sem=precv_sem.at[part],
            device_id=device(me, facing), device_id_type=MESH)

    core_rows = width // 2
    direct, by_pair = width // 4, width // 8
    pair_base = direct

    def some_rows(start, size):
        return pl.ds(pl.multiple_of(start, 16), size)

    def side_of(col_side, x_side, y_side):
        target = jnp.where(col_side == 0, x_side, 1 - x_side)
        return pl.ds(pl.multiple_of((target * y_count + y_side) * cols, cols), cols)

    def w_copy(kind, col_side, to):
        size = (direct, by_pair)[kind]
        start = core * core_rows + (0, pair_base + x_lo * by_pair)[kind]
        return pltpu.make_async_remote_copy(
            src_ref=w_ref.at[:, some_rows(start, size), side_of(col_side, x_hi, to)],
            dst_ref=wall.at[:, y, some_rows(start, size), pl.ds(col_side * cols, cols)],
            send_sem=wsend_sem.at[kind], recv_sem=wrecv_sem.at[kind],
            device_id=device(me, x_hi * y_count + to), device_id_type=MESH)

    def all_w(kind):
        size = (direct, by_pair)[kind]
        block = wall.at[:, pl.ds(0, y_count - 1), pl.ds(0, size)]
        return pltpu.make_async_remote_copy(
            src_ref=block, dst_ref=block, send_sem=wsend_sem.at[kind], recv_sem=wrecv_sem.at[kind],
            device_id=device(me, facing), device_id_type=MESH)

    def w_pass(route, slot, start, size, seq_to):
        block = wall.at[:, slot, some_rows(start, size)]
        return pltpu.make_async_remote_copy(
            src_ref=block, dst_ref=block, send_sem=fsend_sem.at[route], recv_sem=frecv_sem.at[route],
            device_id=device(seq_to, chan), device_id_type=MESH)

    def pass_pair(slot):
        return w_pass(0, slot, core * core_rows + pair_base + x_lo * by_pair, by_pair, mate)

    def pass_core(slot):
        return w_pass(1, slot, core * core_rows, core_rows, sibling)

    def all_pass(route):
        block = wall.at[:, pl.ds(0, y_count - 1), pl.ds(0, (by_pair, core_rows)[route])]
        return pltpu.make_async_remote_copy(
            src_ref=block, dst_ref=block, send_sem=fsend_sem.at[route], recv_sem=frecv_sem.at[route],
            device_id=device((mate, sibling)[route], chan), device_id_type=MESH)

    def own_copy(col_side):
        return pltpu.make_async_copy(
            w_ref.at[:, :, side_of(col_side, x_hi, y)],
            wall.at[:, y, :, pl.ds(col_side * cols, cols)], wown_sem.at[col_side])

    def start_w(kind):
        @pl.loop(1, y_count)
        def _(j):
            for col_side in range(2):
                w_copy(kind, col_side, y_peer(j)).start()

    def share_w():
        all_w(1).wait_recv()

        @pl.loop(1, y_count)
        def _(j):
            pass_pair(y_peer(j)).start()

    def finish_w():
        all_w(0).wait_recv()
        all_pass(0).wait_recv()

        @pl.loop(1, y_count)
        def _(j):
            pass_core(y_peer(j)).start()

        own_copy(0).wait()
        own_copy(1).wait()
        all_pass(1).wait_recv()

    def start_blocks(n):
        @pl.loop(1, seq_count)
        def _(j):
            to = (me + j) % seq_count
            block_copy(n, to, me, to).start()
        recv[n, me] = send[n, me]

    others = pl.ds(0, seq_count - 1)

    def all_blocks(n):
        return block_copy(n, others, others, me)

    def all_back(n):
        return back_copy(n, others, others, me)

    def convolve(n, between=None):
        all_blocks(n).wait_recv()

        for g in range(groups):
            staged[g] = recv[n, :, :, g * LANES:(g + 1) * LANES].astype(F32).reshape(seq_count * 2 * per, LANES)

        def gather_rows(row):
            parts = [staged[g, pl.ds(row, seq_count, stride=2 * per)] for g in range(groups)]
            return jnp.concatenate(parts, axis=0)

        def spectrum(row):
            signal = jnp.concatenate((gather_rows(row), gather_rows(row + per)), axis=1).astype(BF16)
            stage = mm(first_ref[...], jnp.concatenate((signal, signal), axis=0))
            cosine = jnp.concatenate((turns_ref[0], turns_ref[0]), axis=1)
            sine = jnp.concatenate((turns_ref[1], turns_ref[1]), axis=1)
            real, imag = stage[:coarse], stage[coarse:]
            turned_re = real * cosine + imag * sine
            turned_im = imag * cosine - real * sine
            joined = jnp.concatenate((
                jnp.concatenate((turned_re[:, :LANES], turned_im[:, :LANES]), axis=1),
                jnp.concatenate((turned_re[:, LANES:], turned_im[:, LANES:]), axis=1)), axis=0)
            high, low = split(joined)
            both = mm(high, inner_ref[0]) + mm(low, inner_ref[0]) + mm(high, inner_ref[1])
            p_re, p_im = both[:coarse, :LANES], both[:coarse, LANES:]
            h_re, h_im = both[coarse:, :LANES], both[coarse:, LANES:]
            return jnp.concatenate((p_re * h_re - p_im * h_im, p_re * h_im + p_im * h_re), axis=1)

        def pair(step):
            first = 2 * step
            spectra = jnp.concatenate((spectrum(first), spectrum(first + 1)), axis=0)
            high, low = split(spectra)
            back = mm(high, inner_ref[2]) + mm(low, inner_ref[2]) + mm(high, inner_ref[3])
            cosine = jnp.concatenate((turns_ref[0], turns_ref[0]), axis=0)
            sine = jnp.concatenate((turns_ref[1], turns_ref[1]), axis=0)
            real, imag = back[:, :LANES], back[:, LANES:]
            turned_re = real * cosine - imag * sine
            turned_im = imag * cosine + real * sine
            joined = jnp.concatenate((
                jnp.concatenate((turned_re[:coarse], turned_re[coarse:]), axis=1),
                jnp.concatenate((turned_im[:coarse], turned_im[coarse:]), axis=1)), axis=0)
            high, low = split(joined)
            result = mm(last_ref[0], high) + mm(last_ref[0], low) + mm(last_ref[1], high)
            for c in range(2):
                for g in range(groups):
                    ybuf[g % 2, pl.ds((g // 2) * per + first + c, seq_count, stride=2 * per)] = (
                        result[g * seq_count:(g + 1) * seq_count, c * LANES:(c + 1) * LANES])

        steps = per // 2
        for step in range(steps):
            if between is not None and step == steps // 2:
                between()
            pair(step)

        for g in range(2):
            ysend[n, :, :, g * LANES:(g + 1) * LANES] = ybuf[g].astype(BF16).reshape(seq_count, 2 * per, LANES)

        @pl.loop(1, seq_count)
        def _(j):
            to = (me + j) % seq_count
            back_copy(n, to, me, to).start()
        yrecv[n, me] = ysend[n, me]

    def gate(n):
        all_back(n).wait_recv()

        cut = slice(n * width, (n + 1) * width)
        unit = eye(half)
        arrived = yrecv[n].astype(F32).reshape(seq_count, 2, per, half)
        lanes = pl.ds(pl.multiple_of(y * width, width), width)
        for part in range(2):
            at = slice(part * half, (part + 1) * half)
            conv = mm_nt(unit, arrived[:, part].reshape(width, half).astype(BF16))
            product = k_ref[at, cut].astype(F32) * v_ref[at, cut].astype(F32)
            gated = q_ref[at, cut].astype(F32) * (conv + skip_ref[:, cut] * product)
            gall[n, at, lanes] = gated.astype(BF16)

        for part in range(PARTS):
            @pl.loop(1, y_count)
            def _(j):
                gated_copy(n, part, lanes, y_peer(j)).start()

    def wait_gated(n, part):
        all_gated(n, part).wait_recv()

    tile = min(cols, 512)
    tiles = cols // tile

    def term(n, at, lanes):
        return mm(gall[n, at], wall[n, :, :, lanes].reshape(y_count * width, tile))

    def tile_at(side, step):
        return pl.ds(pl.multiple_of(side * cols + step * tile, tile), tile)

    def rows_of(part, size):
        return slice(part * size, (part + 1) * size)

    def own_out(part):
        at = pl.ds(part * half, half)
        return pltpu.make_async_copy(acc.at[at], own_ref.at[at], own_sem.at[part])

    def project_first():
        for part in range(PARTS):
            wait_gated(0, part)

        @pl.loop(0, tiles)
        def _(step):
            acc[:, tile_at(0, step)] = term(0, slice(None), tile_at(1, step))

    def project_last():
        for part in range(PARTS):
            at = rows_of(part, part_rows)
            wait_gated(1, part)

            @pl.loop(0, tiles)
            def _(step):
                psend[at, tile_at(0, step)] = (acc[at, tile_at(0, step)] + term(1, at, tile_at(1, step))).astype(BF16)

            partial_copy(part).start()

        for part in range(2):
            at = rows_of(part, half)

            @pl.loop(0, tiles)
            def _(step):
                acc[at, tile_at(0, step)] = term(0, at, tile_at(0, step)) + term(1, at, tile_at(0, step))

            own_out(part).start()

        for part in range(2):
            own_out(part).wait()
        for part in range(PARTS):
            partial_copy(part).wait_recv()

    start_blocks(0)
    prepare(1)
    start_blocks(1)
    start_w(1)
    start_w(0)
    own_copy(0).start()
    own_copy(1).start()
    for load in loads[3:]:
        load.wait()
    convolve(0)
    share_w()
    convolve(1, lambda: gate(0))
    finish_w()
    gate(1)
    project_first()
    project_last()

    for n in range(CHUNKS):
        all_blocks(n).wait_send()
        all_back(n).wait_send()

    for n in range(CHUNKS):
        for part in range(PARTS):
            all_gated(n, part).wait_send()
    for kind in range(2):
        all_w(kind).wait_send()
        all_pass(kind).wait_send()
    for part in range(PARTS):
        partial_copy(part).wait_send()


def on_device(seq_count, chan_count, query_rows, key_rows, value_rows, filter_taps, skip_gain, w_out):
    rows, channels = query_rows.shape
    cols = w_out.shape[1] // chan_count
    width = channels // CHUNKS
    per = width // seq_count
    y_count = chan_count // 2
    tables = [jnp.asarray(t) for t in transform_tables(seq_count, rows // LANES)]
    anywhere = pl.BlockSpec(memory_space=pl.ANY)
    dma = pltpu.SemaphoreType.DMA
    operands = (query_rows, key_rows, value_rows, filter_taps, skip_gain.reshape(1, channels))
    own, other = pl.pallas_call(
        functools.partial(kernel, seq_count, chan_count),
        out_shape=(jax.ShapeDtypeStruct((rows, cols), F32), jax.ShapeDtypeStruct((rows, cols), BF16)),
        in_specs=[anywhere] * 10,
        out_specs=(anywhere, anywhere),
        scratch_shapes=[
            *(pltpu.VMEM(x.shape, x.dtype) for x in (*operands, *tables)),
            dma((9,)),
            pltpu.VMEM((CHUNKS, seq_count, 2 * per, rows), BF16),
            pltpu.VMEM((CHUNKS, seq_count, 2 * per, rows), BF16),
            pltpu.VMEM((rows // LANES, seq_count * 2 * per, LANES), F32),
            pltpu.VMEM((CHUNKS, seq_count, 2 * per, rows // 2), BF16),
            pltpu.VMEM((CHUNKS, seq_count, 2 * per, rows // 2), BF16),
            pltpu.VMEM((2, seq_count * 2 * per, LANES), F32),
            pltpu.VMEM((CHUNKS, rows, y_count * width), BF16),
            pltpu.VMEM((CHUNKS, y_count, width, 2 * cols), BF16),
            pltpu.VMEM((rows, cols), F32),
            pltpu.VMEM((rows, cols), BF16),
            dma((CHUNKS,)), dma((CHUNKS,)), dma((CHUNKS,)), dma((CHUNKS,)),
            dma((CHUNKS, PARTS)), dma((CHUNKS, PARTS)), dma((PARTS,)), dma((PARTS,)),
            dma((2,)), dma((2,)), dma((2,)), dma((2,)), dma((2,)), dma((2,)),
        ],
        compiler_params=pltpu.CompilerParams(
            collective_id=0, has_side_effects=True, vmem_limit_bytes=56 * 1024 * 1024),
    )(*operands, w_out.reshape(CHUNKS, width, w_out.shape[1]), *tables)
    return (own + other.astype(F32)).astype(BF16)


def solution(mesh):
    return jax.shard_map(
        functools.partial(on_device, mesh.shape["seq"], mesh.shape["chan"]),
        mesh=mesh,
        in_specs=(
            P("seq", "chan"),
            P("seq", "chan"),
            P("seq", "chan"),
            P("seq", "chan"),
            P("chan"),
            P("chan", None),
        ),
        out_specs=P("seq", "chan"),
        check_vma=False,
    )
```

```python
import functools

import jax
import jax.numpy as jnp
import ml_dtypes
import numpy as np
from jax import lax
from jax.experimental import pallas as pl
from jax.experimental.pallas import tpu as pltpu
from jax.sharding import PartitionSpec as P

MESH = pl.DeviceIdType.MESH
LANES = 128
CHUNKS = 4
PARTS = 4
BF16 = jnp.bfloat16
F32 = jnp.float32


def split_table(table):
    high = table.astype(ml_dtypes.bfloat16)
    low = (table - high.astype(np.float64)).astype(ml_dtypes.bfloat16)
    return high, low


def transform_tables(seq_count, row_groups):
    coarse = seq_count * row_groups
    total = coarse * LANES
    freq = np.arange(coarse) + 0.25
    order = (np.arange(seq_count)[None, :] * row_groups + np.arange(row_groups)[:, None]).reshape(-1)
    angle = 2.0 * np.pi * freq[:, None] * order[None, :] / coarse
    forward_first = np.concatenate((np.cos(angle), -np.sin(angle)), axis=0)
    inverse_first = np.concatenate((np.cos(angle).T, -np.sin(angle).T), axis=1) / total
    fine = np.arange(LANES)
    turn = 2.0 * np.pi * freq[:, None] * fine[None, :] / total
    twist_cos = np.cos(turn).astype(np.float32)
    twist_sin = np.sin(turn).astype(np.float32)
    inner = 2.0 * np.pi * (fine[:, None] * fine[None, :] % LANES) / LANES
    cosine, sine = np.cos(inner), np.sin(inner)
    forward_second = np.block([[cosine, -sine], [sine, cosine]])
    inverse_second = np.block([[cosine, sine], [-sine, cosine]])
    turns = np.stack((twist_cos, twist_sin))
    inner = np.stack((*split_table(forward_second), *split_table(inverse_second)))
    first = np.concatenate(split_table(forward_first), axis=1)
    last = np.stack(split_table(inverse_first))
    return turns, inner, first, last


def mm(left, right):
    return jnp.dot(left, right, preferred_element_type=F32)


def mm_nt(left, right):
    return lax.dot_general(left, right, (((1,), (1,)), ((), ())), preferred_element_type=F32)


def split(value):
    high = value.astype(BF16)
    low = (value - high.astype(F32)).astype(BF16)
    return high, low


def eye(size):
    row = lax.broadcasted_iota(jnp.int32, (size, size), 0)
    col = lax.broadcasted_iota(jnp.int32, (size, size), 1)
    return (row == col).astype(F32).astype(BF16)


def by_owner(seq_count, per):
    width = seq_count * per
    row = lax.broadcasted_iota(jnp.int32, (2 * width, 2 * width), 0)
    col = lax.broadcasted_iota(jnp.int32, (2 * width, 2 * width), 1)
    picked = row // per % 2 * width + row % per * seq_count + row // (2 * per)
    return (picked == col).astype(F32).astype(BF16)


def kernel(
    seq_count, chan_count,
    q_hbm, k_hbm, v_hbm, h_hbm, skip_hbm, w_ref, turns_hbm, inner_hbm, first_hbm, last_hbm,
    own_ref, precv,
    q_ref, k_ref, v_ref, h_ref, skip_ref, turns_ref, inner_ref, first_ref, last_ref, load_sem,
    send, recv, staged, zhi, zlo, yhi, ylo, ehi, elo, ysend, yrecv, ybuf, gall, wall, psend,
    send_sem, recv_sem, ysend_sem, yrecv_sem, gsend_sem, grecv_sem, psend_sem, precv_sem,
    wsend_sem, wrecv_sem, fsend_sem, frecv_sem, wown_sem,
):
    rows, channels = q_ref.shape
    groups = rows // LANES
    width = channels // CHUNKS
    per = width // seq_count
    coarse = seq_count * groups
    cols = own_ref.shape[1]
    y_count = chan_count // 2
    half = rows // 2
    levels = seq_count // 4
    part_rows = rows // PARTS
    me = lax.axis_index("seq")
    chan = lax.axis_index("chan")
    core = me % 2
    x_lo = (me // 2) % 2
    sibling = me + 1 - 2 * core
    mate = me + 2 - 4 * x_lo
    x_hi = chan // y_count
    y = chan % y_count
    facing = (1 - x_hi) * y_count + y

    def y_peer(j):
        return (y + j) % y_count

    def partner(j):
        group = (j + j // (seq_count - 4)) // 4
        shift = (group // 2 + 1) * (1 - 2 * (group % 2)) * (1 - group // (levels - 1))
        turn = (j + j // (seq_count - 4)) % 4
        return (me // 4 + shift + levels) % levels * 4 + (me % 4 + turn) % 4

    def device(seq_to, chan_to):
        return {"seq": seq_to, "chan": chan_to}

    barrier = pltpu.get_barrier_semaphore()

    @pl.loop(1, seq_count)
    def _(j):
        pl.semaphore_signal(barrier, inc=1, device_id=device((me + j) % seq_count, chan), device_id_type=MESH)

    @pl.loop(1, y_count)
    def _(j):
        pl.semaphore_signal(barrier, inc=1, device_id=device(me, x_hi * y_count + y_peer(j)), device_id_type=MESH)

    pl.semaphore_signal(barrier, inc=1, device_id=device(me, facing), device_id_type=MESH)

    loads = [pltpu.make_async_copy(source, target, load_sem.at[i]) for i, (source, target) in enumerate((
        (k_hbm, k_ref), (v_hbm, v_ref), (h_hbm, h_ref), (turns_hbm, turns_ref), (inner_hbm, inner_ref),
        (first_hbm, first_ref), (last_hbm, last_ref), (q_hbm, q_ref), (skip_hbm, skip_ref)))]
    for load in loads:
        load.start()
    for load in loads[:3]:
        load.wait()

    def prepare(n):
        cut = slice(n * width, (n + 1) * width)
        product = (k_ref[:, cut].astype(F32) * v_ref[:, cut].astype(F32)).astype(BF16)
        both = jnp.concatenate((product, h_ref[:, cut].astype(BF16)), axis=1)
        ordered = mm_nt(by_owner(seq_count, per), both).reshape(seq_count, 2 * per, rows)
        send[n] = jnp.concatenate((ordered[:, :, :half], ordered[:, :, half:]), axis=1).astype(BF16)

    prepare(0)
    pl.semaphore_wait(barrier, seq_count + y_count - 1)

    def block_copy(n, slot_out, slot_in, to):
        return pltpu.make_async_remote_copy(
            src_ref=send.at[n, slot_out], dst_ref=recv.at[n, slot_in],
            send_sem=send_sem.at[n], recv_sem=recv_sem.at[n],
            device_id={"seq": to, "chan": chan}, device_id_type=MESH)

    def back_copy(n, slot_out, slot_in, to):
        return pltpu.make_async_remote_copy(
            src_ref=ysend.at[n, slot_out], dst_ref=yrecv.at[n, slot_in],
            send_sem=ysend_sem.at[n], recv_sem=yrecv_sem.at[n],
            device_id={"seq": to, "chan": chan}, device_id_type=MESH)

    def gated_copy(n, part, lanes, to):
        block = gall.at[pl.ds(part * part_rows, part_rows), lanes]
        return pltpu.make_async_remote_copy(
            src_ref=block, dst_ref=block,
            send_sem=gsend_sem.at[n, part], recv_sem=grecv_sem.at[n, part],
            device_id=device(me, x_hi * y_count + to), device_id_type=MESH)

    def all_gated(n, part):
        return gated_copy(n, part, pl.ds(0, (y_count - 1) * width), y)

    def partial_copy(part):
        at = pl.ds(part * part_rows, part_rows)
        return pltpu.make_async_remote_copy(
            src_ref=psend.at[at], dst_ref=precv.at[at],
            send_sem=psend_sem.at[part], recv_sem=precv_sem.at[part],
            device_id=device(me, facing), device_id_type=MESH)

    core_rows = width // 2
    by_pair = width // 8
    first_half, last_half = pl.ds(0, CHUNKS // 2), pl.ds(CHUNKS // 2, CHUNKS // 2)
    w_chunks = (pl.ds(0, CHUNKS), pl.ds(0, CHUNKS), first_half, last_half)
    w_rows = (by_pair, core_rows - 2 * by_pair, core_rows // 2, core_rows)
    w_side = (1, 1, 0, 0)

    def w_start(kind):
        return core * core_rows + (x_lo * by_pair, 2 * by_pair, x_lo * (core_rows // 2), 0)[kind]

    def some_rows(start, size):
        return pl.ds(pl.multiple_of(start, 16), size)

    def lanes_of(side):
        return pl.ds(side * cols, cols)

    def side_of(col_side, x_side, y_side):
        target = jnp.where(col_side == 0, x_side, 1 - x_side)
        return pl.ds(pl.multiple_of((target * y_count + y_side) * cols, cols), cols)

    def w_copy(kind, to):
        at, side = some_rows(w_start(kind), w_rows[kind]), w_side[kind]
        return pltpu.make_async_remote_copy(
            src_ref=w_ref.at[w_chunks[kind], at, side_of(side, x_hi, to)], dst_ref=wall.at[w_chunks[kind], y, at, lanes_of(side)],
            send_sem=wsend_sem.at[kind], recv_sem=wrecv_sem.at[kind],
            device_id=device(me, x_hi * y_count + to), device_id_type=MESH)

    def all_w(kind):
        block = wall.at[w_chunks[kind], pl.ds(0, y_count - 1), pl.ds(0, w_rows[kind]), lanes_of(0)]
        return pltpu.make_async_remote_copy(
            src_ref=block, dst_ref=block, send_sem=wsend_sem.at[kind], recv_sem=wrecv_sem.at[kind],
            device_id=device(me, facing), device_id_type=MESH)

    pass_rows = (by_pair, core_rows // 2, core_rows, core_rows, core_rows)
    pass_side = (1, 0, 1, 0, 0)
    pass_chunks = (pl.ds(0, CHUNKS), first_half, pl.ds(0, CHUNKS), first_half, last_half)
    pass_to = (mate, mate, sibling, sibling, sibling)

    def w_pass(route, slot):
        start = core * core_rows + (x_lo * pass_rows[route] if route < 2 else 0)
        block = wall.at[pass_chunks[route], slot, some_rows(start, pass_rows[route]), lanes_of(pass_side[route])]
        return pltpu.make_async_remote_copy(
            src_ref=block, dst_ref=block, send_sem=fsend_sem.at[route], recv_sem=frecv_sem.at[route],
            device_id=device(pass_to[route], chan), device_id_type=MESH)

    def all_pass(route):
        block = wall.at[pass_chunks[route], pl.ds(0, y_count - 1), pl.ds(0, pass_rows[route]), lanes_of(0)]
        return pltpu.make_async_remote_copy(
            src_ref=block, dst_ref=block, send_sem=fsend_sem.at[route], recv_sem=frecv_sem.at[route],
            device_id=device(pass_to[route], chan), device_id_type=MESH)

    def own_copy(col_side):
        return pltpu.make_async_copy(
            w_ref.at[:, :, side_of(col_side, x_hi, y)],
            wall.at[:, y, :, pl.ds(col_side * cols, cols)], wown_sem.at[col_side])

    def start_w(kind):
        @pl.loop(1, y_count)
        def _(j):
            w_copy(kind, y_peer(j)).start()

    def start_pass(route):
        @pl.loop(1, y_count)
        def _(j):
            w_pass(route, y_peer(j)).start()

    def start_blocks(n):
        @pl.loop(0, seq_count - 1)
        def _(j):
            to = partner(j)
            block_copy(n, to, me, to).start()
        recv[n, me] = send[n, me]

    others = pl.ds(0, seq_count - 1)

    def all_blocks(n):
        return block_copy(n, others, others, me)

    def all_back(n):
        return back_copy(n, others, others, me)

    def convolve(n):
        all_blocks(n).wait_recv()
        if n + 2 < CHUNKS:
            start_blocks(n + 2)

        for g in range(2):
            staged[g] = recv[n, :, :, g * LANES:(g + 1) * LANES].astype(F32).reshape(seq_count * 4 * per, LANES)

        def gather_rows(row):
            parts = [staged[g % 2, pl.ds(g // 2 * 2 * per + row, seq_count, stride=4 * per)] for g in range(groups)]
            return jnp.concatenate(parts, axis=0)

        cosine, sine = turns_ref[0], turns_ref[1]
        cosines, sines = jnp.concatenate((cosine, cosine), axis=1), jnp.concatenate((sine, sine), axis=1)
        for c in range(per):
            signal = jnp.concatenate((gather_rows(c), gather_rows(c + per)), axis=1).astype(BF16)
            stage = mm(first_ref[...], jnp.concatenate((signal, signal), axis=0))
            real, imag = stage[:coarse], stage[coarse:]
            turned_re = real * cosines + imag * sines
            turned_im = imag * cosines - real * sines
            for side in range(2):
                at = slice((2 * c + side) * coarse, (2 * c + side + 1) * coarse)
                lanes = slice(side * LANES, (side + 1) * LANES)
                zhi[at, :LANES], zlo[at, :LANES] = split(turned_re[:, lanes])
                zhi[at, LANES:], zlo[at, LANES:] = split(turned_im[:, lanes])

        group = min(per, 4)
        for t in range(per // group):
            at = slice(2 * group * t * coarse, 2 * group * (t + 1) * coarse)
            high, low = zhi[at], zlo[at]
            both = mm(high, inner_ref[0]) + mm(low, inner_ref[0]) + mm(high, inner_ref[1])
            for c in range(group):
                p_re, p_im = both[2 * c * coarse:(2 * c + 1) * coarse, :LANES], both[2 * c * coarse:(2 * c + 1) * coarse, LANES:]
                h_re, h_im = both[(2 * c + 1) * coarse:(2 * c + 2) * coarse, :LANES], both[(2 * c + 1) * coarse:(2 * c + 2) * coarse, LANES:]
                at = slice((t * group + c) * coarse, (t * group + c + 1) * coarse)
                yhi[at, :LANES], ylo[at, :LANES] = split(p_re * h_re - p_im * h_im)
                yhi[at, LANES:], ylo[at, LANES:] = split(p_re * h_im + p_im * h_re)

        for t in range(per // group):
            at = slice(group * t * coarse, group * (t + 1) * coarse)
            high, low = yhi[at], ylo[at]
            back = mm(high, inner_ref[2]) + mm(low, inner_ref[2]) + mm(high, inner_ref[3])
            for c in range(group):
                real, imag = back[c * coarse:(c + 1) * coarse, :LANES], back[c * coarse:(c + 1) * coarse, LANES:]
                lanes = slice((t * group + c) * LANES, (t * group + c + 1) * LANES)
                ehi[:coarse, lanes], elo[:coarse, lanes] = split(real * cosine - imag * sine)
                ehi[coarse:, lanes], elo[coarse:, lanes] = split(imag * cosine + real * sine)

        for t in range(per // group):
            lanes = slice(group * t * LANES, group * (t + 1) * LANES)
            high, low = ehi[:, lanes], elo[:, lanes]
            result = mm(last_ref[0], high) + mm(last_ref[0], low) + mm(last_ref[1], high)
            for c in range(group):
                for g in range(groups):
                    ybuf[pl.ds(g * per + t * group + c, seq_count, stride=4 * per)] = (
                        result[g * seq_count:(g + 1) * seq_count, c * LANES:(c + 1) * LANES])

        ysend[n] = ybuf[...].astype(BF16).reshape(seq_count, 4 * per, LANES)

        @pl.loop(0, seq_count - 1)
        def _(j):
            to = partner(j)
            back_copy(n, to, me, to).start()
        yrecv[n, me] = ysend[n, me]

    def gate(n):
        all_back(n).wait_recv()

        cut = slice(n * width, (n + 1) * width)
        ybuf[...] = yrecv[n].astype(F32).reshape(seq_count * 4 * per, LANES)
        arrived = [ybuf[pl.ds(row, seq_count, stride=4 * per)] for row in range(4 * per)]
        turned = mm_nt(eye(LANES), jnp.concatenate(arrived, axis=0).astype(BF16))
        lanes = pl.ds(pl.multiple_of(n * y_count * width + y * width, width), width)
        for g in range(groups):
            at = slice(g * LANES, (g + 1) * LANES)
            product = k_ref[at, cut].astype(F32) * v_ref[at, cut].astype(F32)
            conv = turned[:, g * width:(g + 1) * width]
            gated = q_ref[at, cut].astype(F32) * (conv + skip_ref[:, cut] * product)
            gall[at, lanes] = gated.astype(BF16)

    def send_gated(n, part):
        lanes = pl.ds(pl.multiple_of(n * y_count * width + y * width, width), width)

        @pl.loop(1, y_count)
        def _(j):
            gated_copy(n, part, lanes, y_peer(j)).start()

    def wait_gated(n, part):
        all_gated(n, part).wait_recv()

    tile = min(cols, 512)
    tiles = cols // tile

    depth = y_count * width

    def term(first, last, at, lanes):
        left = gall[at, first * depth:last * depth]
        return mm(left, wall[first:last, :, :, lanes].reshape((last - first) * depth, tile))

    def tile_at(side, step):
        return pl.ds(pl.multiple_of(side * cols + step * tile, tile), tile)

    def rows_of(part, size):
        return slice(part * size, (part + 1) * size)

    def project_other(part):
        at = rows_of(part, part_rows)
        for n in range(CHUNKS):
            wait_gated(n, part)

        @pl.loop(0, tiles)
        def _(step):
            psend[at, tile_at(0, step)] = term(0, CHUNKS, at, tile_at(1, step)).astype(BF16)

        partial_copy(part).start()

    def project_own():
        own_copy(0).wait()
        all_pass(3).wait_recv()
        for part in range(2):
            at = rows_of(part, half)

            @pl.loop(0, tiles)
            def _(step):
                own_ref[at, tile_at(0, step)] = term(0, CHUNKS // 2, at, tile_at(0, step))

        all_w(3).wait_recv()
        start_pass(4)
        all_pass(4).wait_recv()
        for part in range(2):
            at = rows_of(part, half)

            @pl.loop(0, tiles)
            def _(step):
                own_ref[at, tile_at(0, step)] += term(CHUNKS // 2, CHUNKS, at, tile_at(0, step))

    start_blocks(0)
    prepare(1)
    start_blocks(1)
    start_w(0)
    start_w(1)
    start_w(2)
    own_copy(1).start()
    own_copy(0).start()
    for n in range(2, CHUNKS):
        prepare(n)
    for load in loads[3:]:
        load.wait()
    convolve(0)
    all_w(0).wait_recv()
    start_pass(0)
    convolve(1)
    convolve(2)
    gate(0)
    for part in range(PARTS):
        send_gated(0, part)
    convolve(3)
    all_w(2).wait_recv()
    start_pass(1)
    all_w(1).wait_recv()
    all_pass(0).wait_recv()
    start_pass(2)
    gate(1)
    for part in range(3):
        send_gated(1, part)
    gate(2)
    for part in range(2):
        send_gated(2, part)
    gate(3)
    for n, part in ((3, 0), (3, 1), (2, 2), (3, 2), (1, 3), (2, 3), (3, 3)):
        send_gated(n, part)
    start_w(3)
    all_pass(1).wait_recv()
    start_pass(3)
    own_copy(1).wait()
    all_pass(2).wait_recv()
    for part in range(PARTS):
        project_other(part)
    project_own()
    for part in range(PARTS):
        partial_copy(part).wait_recv()

    for n in range(CHUNKS):
        all_blocks(n).wait_send()
        all_back(n).wait_send()

    for n in range(CHUNKS):
        for part in range(PARTS):
            all_gated(n, part).wait_send()
    for kind in range(4):
        all_w(kind).wait_send()
    for route in range(5):
        all_pass(route).wait_send()
    for part in range(PARTS):
        partial_copy(part).wait_send()


def on_device(seq_count, chan_count, query_rows, key_rows, value_rows, filter_taps, skip_gain, w_out):
    rows, channels = query_rows.shape
    cols = w_out.shape[1] // chan_count
    width = channels // CHUNKS
    per = width // seq_count
    y_count = chan_count // 2
    coarse = seq_count * rows // LANES
    tables = [jnp.asarray(t) for t in transform_tables(seq_count, rows // LANES)]
    anywhere = pl.BlockSpec(memory_space=pl.ANY)
    dma = pltpu.SemaphoreType.DMA
    operands = (query_rows, key_rows, value_rows, filter_taps, skip_gain.reshape(1, channels))
    own, other = pl.pallas_call(
        functools.partial(kernel, seq_count, chan_count),
        out_shape=(pltpu.VMEM((rows, cols), F32), pltpu.VMEM((rows, cols), BF16)),
        in_specs=[anywhere] * 10,
        out_specs=(pl.BlockSpec(memory_space=pltpu.VMEM),) * 2,
        scratch_shapes=[
            *(pltpu.VMEM(x.shape, x.dtype) for x in (*operands, *tables)),
            dma((9,)),
            pltpu.VMEM((CHUNKS, seq_count, 4 * per, rows // 2), BF16),
            pltpu.VMEM((CHUNKS, seq_count, 4 * per, rows // 2), BF16),
            pltpu.VMEM((2, seq_count * 4 * per, LANES), F32),
            *(pltpu.VMEM((2 * per * coarse, 2 * LANES), BF16) for _ in range(2)),
            *(pltpu.VMEM((per * coarse, 2 * LANES), BF16) for _ in range(2)),
            *(pltpu.VMEM((2 * coarse, per * LANES), BF16) for _ in range(2)),
            pltpu.VMEM((CHUNKS, seq_count, 4 * per, LANES), BF16),
            pltpu.VMEM((CHUNKS, seq_count, 4 * per, LANES), BF16),
            pltpu.VMEM((seq_count * 4 * per, LANES), F32),
            pltpu.VMEM((rows, CHUNKS * y_count * width), BF16),
            pltpu.VMEM((CHUNKS, y_count, width, 2 * cols), BF16),
            pltpu.VMEM((rows, cols), BF16),
            dma((CHUNKS,)), dma((CHUNKS,)), dma((CHUNKS,)), dma((CHUNKS,)),
            dma((CHUNKS, PARTS)), dma((CHUNKS, PARTS)), dma((PARTS,)), dma((PARTS,)),
            dma((4,)), dma((4,)), dma((5,)), dma((5,)), dma((2,)),
        ],
        compiler_params=pltpu.CompilerParams(
            collective_id=0, has_side_effects=True, vmem_limit_bytes=56 * 1024 * 1024),
    )(*operands, w_out.reshape(CHUNKS, width, w_out.shape[1]), *tables)
    return (own + other.astype(F32)).astype(BF16)


def solution(mesh):
    return jax.shard_map(
        functools.partial(on_device, mesh.shape["seq"], mesh.shape["chan"]),
        mesh=mesh,
        in_specs=(
            P("seq", "chan"),
            P("seq", "chan"),
            P("seq", "chan"),
            P("seq", "chan"),
            P("chan"),
            P("chan", None),
        ),
        out_specs=P("seq", "chan"),
        check_vma=False,
    )
```

```python
import functools

import jax
import jax.numpy as jnp
import ml_dtypes
import numpy as np
from jax import lax
from jax.experimental import pallas as pl
from jax.experimental.pallas import tpu as pltpu
from jax.sharding import PartitionSpec as P

MESH = pl.DeviceIdType.MESH
LANES = 128
CHUNKS = 4
PARTS = 4
BF16 = jnp.bfloat16
F32 = jnp.float32


def split_table(table):
    high = table.astype(ml_dtypes.bfloat16)
    low = (table - high.astype(np.float64)).astype(ml_dtypes.bfloat16)
    return high, low


def transform_tables(seq_count, row_groups):
    coarse = seq_count * row_groups
    total = coarse * LANES
    freq = np.arange(coarse) + 0.25
    order = (np.arange(seq_count)[None, :] * row_groups + np.arange(row_groups)[:, None]).reshape(-1)
    angle = 2.0 * np.pi * freq[:, None] * order[None, :] / coarse
    forward_first = np.concatenate((np.cos(angle), -np.sin(angle)), axis=0)
    inverse_first = np.concatenate((np.cos(angle).T, -np.sin(angle).T), axis=1) / total
    fine = np.arange(LANES)
    turn = 2.0 * np.pi * freq[:, None] * fine[None, :] / total
    twist_cos = np.cos(turn).astype(np.float32)
    twist_sin = np.sin(turn).astype(np.float32)
    inner = 2.0 * np.pi * (fine[:, None] * fine[None, :] % LANES) / LANES
    cosine, sine = np.cos(inner), np.sin(inner)
    forward_second = np.block([[cosine, -sine], [sine, cosine]])
    inverse_second = np.block([[cosine, sine], [-sine, cosine]])
    turns = np.stack((twist_cos, twist_sin))
    inner = np.stack((*split_table(forward_second), *split_table(inverse_second)))
    first = np.concatenate(split_table(forward_first), axis=1)
    last = np.stack(split_table(inverse_first))
    return turns, inner, first, last


def mm(left, right):
    return jnp.dot(left, right, preferred_element_type=F32)


def mm_nt(left, right):
    return lax.dot_general(left, right, (((1,), (1,)), ((), ())), preferred_element_type=F32)


def split(value):
    high = value.astype(BF16)
    low = (value - high.astype(F32)).astype(BF16)
    return high, low


def eye(size):
    row = lax.broadcasted_iota(jnp.int32, (size, size), 0)
    col = lax.broadcasted_iota(jnp.int32, (size, size), 1)
    return (row == col).astype(F32).astype(BF16)


def by_owner(seq_count, per):
    width = seq_count * per
    row = lax.broadcasted_iota(jnp.int32, (2 * width, 2 * width), 0)
    col = lax.broadcasted_iota(jnp.int32, (2 * width, 2 * width), 1)
    picked = row // per % 2 * width + row % per * seq_count + row // (2 * per)
    return (picked == col).astype(F32).astype(BF16)


def kernel(
    seq_count, chan_count,
    q_hbm, k_hbm, v_hbm, h_hbm, skip_hbm, w_ref, turns_hbm, inner_hbm, first_hbm, last_hbm,
    own_ref, precv,
    q_ref, k_ref, v_ref, h_ref, skip_ref, turns_ref, inner_ref, first_ref, last_ref, load_sem,
    send, recv, staged, zhi, zlo, yhi, ylo, ehi, elo, ysend, yrecv, ybuf, gall, wall, acc, psend,
    send_sem, recv_sem, ysend_sem, yrecv_sem, gsend_sem, grecv_sem, psend_sem, precv_sem,
    wsend_sem, wrecv_sem, fsend_sem, frecv_sem, wown_sem,
):
    rows, channels = q_ref.shape
    groups = rows // LANES
    width = channels // CHUNKS
    per = width // seq_count
    coarse = seq_count * groups
    cols = own_ref.shape[1]
    y_count = chan_count // 2
    half = rows // 2
    levels = seq_count // 4
    part_rows = rows // PARTS
    me = lax.axis_index("seq")
    chan = lax.axis_index("chan")
    core = me % 2
    x_lo = (me // 2) % 2
    parity = (me // 4) % 2
    above = (me + 4) % seq_count
    below = (me + seq_count - 4) % seq_count
    sibling = me + 1 - 2 * core
    mate = me + 2 - 4 * x_lo
    x_hi = chan // y_count
    y = chan % y_count
    facing = (1 - x_hi) * y_count + y

    def y_peer(j):
        return (y + j) % y_count

    def partner(j):
        group = (j + j // (seq_count - 4)) // 4
        shift = (group // 2 + 1) * (1 - 2 * (group % 2)) * (1 - group // (levels - 1))
        turn = (j + j // (seq_count - 4)) % 4
        return (me // 4 + shift + levels) % levels * 4 + (me % 4 + turn) % 4

    def device(seq_to, chan_to):
        return {"seq": seq_to, "chan": chan_to}

    barrier = pltpu.get_barrier_semaphore()

    @pl.loop(1, seq_count)
    def _(j):
        pl.semaphore_signal(barrier, inc=1, device_id=device((me + j) % seq_count, chan), device_id_type=MESH)

    @pl.loop(1, y_count)
    def _(j):
        pl.semaphore_signal(barrier, inc=1, device_id=device(me, x_hi * y_count + y_peer(j)), device_id_type=MESH)

    pl.semaphore_signal(barrier, inc=1, device_id=device(me, facing), device_id_type=MESH)

    loads = [pltpu.make_async_copy(source, target, load_sem.at[i]) for i, (source, target) in enumerate((
        (k_hbm, k_ref), (v_hbm, v_ref), (h_hbm, h_ref), (turns_hbm, turns_ref), (inner_hbm, inner_ref),
        (first_hbm, first_ref), (last_hbm, last_ref), (q_hbm, q_ref), (skip_hbm, skip_ref)))]
    for load in loads:
        load.start()
    for load in loads[:3]:
        load.wait()

    def prepare(n):
        cut = slice(n * width, (n + 1) * width)
        product = (k_ref[:, cut].astype(F32) * v_ref[:, cut].astype(F32)).astype(BF16)
        both = jnp.concatenate((product, h_ref[:, cut].astype(BF16)), axis=1)
        ordered = mm_nt(by_owner(seq_count, per), both).reshape(seq_count, 2 * per, rows)
        send[n] = jnp.concatenate((ordered[:, :, :half], ordered[:, :, half:]), axis=1).astype(BF16)

    prepare(0)
    pl.semaphore_wait(barrier, seq_count + y_count - 1)

    def block_copy(n, slot_out, slot_in, to):
        return pltpu.make_async_remote_copy(
            src_ref=send.at[n, slot_out], dst_ref=recv.at[n, slot_in],
            send_sem=send_sem.at[n], recv_sem=recv_sem.at[n],
            device_id={"seq": to, "chan": chan}, device_id_type=MESH)

    def back_copy(n, slot_out, slot_in, to):
        return pltpu.make_async_remote_copy(
            src_ref=ysend.at[n, slot_out], dst_ref=yrecv.at[n, slot_in],
            send_sem=ysend_sem.at[n], recv_sem=yrecv_sem.at[n],
            device_id={"seq": to, "chan": chan}, device_id_type=MESH)

    def gated_copy(n, part, lanes, to):
        block = gall.at[pl.ds(part * part_rows, part_rows), lanes]
        return pltpu.make_async_remote_copy(
            src_ref=block, dst_ref=block,
            send_sem=gsend_sem.at[n, part], recv_sem=grecv_sem.at[n, part],
            device_id=device(me, x_hi * y_count + to), device_id_type=MESH)

    def all_gated(n, part):
        return gated_copy(n, part, pl.ds(0, (y_count - 1) * width), y)

    def partial_copy(part):
        at = pl.ds(part * part_rows, part_rows)
        return pltpu.make_async_remote_copy(
            src_ref=psend.at[at], dst_ref=precv.at[at],
            send_sem=psend_sem.at[part], recv_sem=precv_sem.at[part],
            device_id=device(me, facing), device_id_type=MESH)

    core_rows = width // 2
    by_pair = width // 8
    first_half, last_half = pl.ds(0, CHUNKS // 2), pl.ds(CHUNKS // 2, CHUNKS // 2)
    w_chunks = (pl.ds(0, CHUNKS), pl.ds(0, CHUNKS), first_half, last_half)
    w_rows = (by_pair, core_rows - 2 * by_pair, core_rows // 2, core_rows // 2)
    w_side = (1, 1, 0, 0)

    def w_start(kind):
        return core * core_rows + (x_lo * by_pair, 2 * by_pair, parity * (core_rows // 2), parity * (core_rows // 2))[kind]

    def some_rows(start, size):
        return pl.ds(pl.multiple_of(start, 16), size)

    def lanes_of(side):
        return pl.ds(side * cols, cols)

    def side_of(col_side, x_side, y_side):
        target = jnp.where(col_side == 0, x_side, 1 - x_side)
        return pl.ds(pl.multiple_of((target * y_count + y_side) * cols, cols), cols)

    def w_copy(kind, to):
        at, side = some_rows(w_start(kind), w_rows[kind]), w_side[kind]
        return pltpu.make_async_remote_copy(
            src_ref=w_ref.at[w_chunks[kind], at, side_of(side, x_hi, to)], dst_ref=wall.at[w_chunks[kind], y, at, lanes_of(side)],
            send_sem=wsend_sem.at[kind], recv_sem=wrecv_sem.at[kind],
            device_id=device(me, x_hi * y_count + to), device_id_type=MESH)

    def all_w(kind):
        block = wall.at[w_chunks[kind], pl.ds(0, y_count - 1), pl.ds(0, w_rows[kind]), lanes_of(0)]
        return pltpu.make_async_remote_copy(
            src_ref=block, dst_ref=block, send_sem=wsend_sem.at[kind], recv_sem=wrecv_sem.at[kind],
            device_id=device(me, facing), device_id_type=MESH)

    quarter = core_rows // 4
    pass_rows = (by_pair, quarter, quarter, quarter, core_rows, core_rows, core_rows, quarter)
    pass_side = (1, 0, 0, 0, 1, 0, 0, 0)
    every = pl.ds(0, CHUNKS)
    pass_chunks = (every, first_half, last_half, last_half, every, first_half, last_half, first_half)
    pass_to = (mate, above, above, below, sibling, sibling, sibling, below)

    def w_pass(route, slot):
        up, down = parity * 2 * quarter, (parity * 2 + 1) * quarter
        start = core * core_rows + (x_lo * by_pair, up, up, down, 0, 0, 0, down)[route]
        block = wall.at[pass_chunks[route], slot, some_rows(start, pass_rows[route]), lanes_of(pass_side[route])]
        return pltpu.make_async_remote_copy(
            src_ref=block, dst_ref=block, send_sem=fsend_sem.at[route], recv_sem=frecv_sem.at[route],
            device_id=device(pass_to[route], chan), device_id_type=MESH)

    def all_pass(route):
        block = wall.at[pass_chunks[route], pl.ds(0, y_count - 1), pl.ds(0, pass_rows[route]), lanes_of(0)]
        return pltpu.make_async_remote_copy(
            src_ref=block, dst_ref=block, send_sem=fsend_sem.at[route], recv_sem=frecv_sem.at[route],
            device_id=device(pass_to[route], chan), device_id_type=MESH)

    def own_copy(col_side):
        return pltpu.make_async_copy(
            w_ref.at[:, :, side_of(col_side, x_hi, y)],
            wall.at[:, y, :, pl.ds(col_side * cols, cols)], wown_sem.at[col_side])

    def start_w(kind):
        @pl.loop(1, y_count)
        def _(j):
            w_copy(kind, y_peer(j)).start()

    def start_pass(route):
        @pl.loop(1, y_count)
        def _(j):
            w_pass(route, y_peer(j)).start()

    def start_blocks(n):
        @pl.loop(0, seq_count - 1)
        def _(j):
            to = partner(j)
            block_copy(n, to, me, to).start()
        recv[n, me] = send[n, me]

    others = pl.ds(0, seq_count - 1)

    def all_blocks(n):
        return block_copy(n, others, others, me)

    def all_back(n):
        return back_copy(n, others, others, me)

    def convolve(n):
        all_blocks(n).wait_recv()
        if n + 2 < CHUNKS:
            start_blocks(n + 2)

        for g in range(2):
            staged[g] = recv[n, :, :, g * LANES:(g + 1) * LANES].astype(F32).reshape(seq_count * 4 * per, LANES)

        def gather_rows(row):
            parts = [staged[g % 2, pl.ds(g // 2 * 2 * per + row, seq_count, stride=4 * per)] for g in range(groups)]
            return jnp.concatenate(parts, axis=0)

        cosine, sine = turns_ref[0], turns_ref[1]
        cosines, sines = jnp.concatenate((cosine, cosine), axis=1), jnp.concatenate((sine, sine), axis=1)
        for c in range(per):
            signal = jnp.concatenate((gather_rows(c), gather_rows(c + per)), axis=1).astype(BF16)
            stage = mm(first_ref[...], jnp.concatenate((signal, signal), axis=0))
            real, imag = stage[:coarse], stage[coarse:]
            turned_re = real * cosines + imag * sines
            turned_im = imag * cosines - real * sines
            for side in range(2):
                at = slice((2 * c + side) * coarse, (2 * c + side + 1) * coarse)
                lanes = slice(side * LANES, (side + 1) * LANES)
                zhi[at, :LANES], zlo[at, :LANES] = split(turned_re[:, lanes])
                zhi[at, LANES:], zlo[at, LANES:] = split(turned_im[:, lanes])

        group = min(per, 4)
        for t in range(per // group):
            at = slice(2 * group * t * coarse, 2 * group * (t + 1) * coarse)
            high, low = zhi[at], zlo[at]
            both = mm(high, inner_ref[0]) + mm(low, inner_ref[0]) + mm(high, inner_ref[1])
            for c in range(group):
                p_re, p_im = both[2 * c * coarse:(2 * c + 1) * coarse, :LANES], both[2 * c * coarse:(2 * c + 1) * coarse, LANES:]
                h_re, h_im = both[(2 * c + 1) * coarse:(2 * c + 2) * coarse, :LANES], both[(2 * c + 1) * coarse:(2 * c + 2) * coarse, LANES:]
                at = slice((t * group + c) * coarse, (t * group + c + 1) * coarse)
                yhi[at, :LANES], ylo[at, :LANES] = split(p_re * h_re - p_im * h_im)
                yhi[at, LANES:], ylo[at, LANES:] = split(p_re * h_im + p_im * h_re)

        for t in range(per // group):
            at = slice(group * t * coarse, group * (t + 1) * coarse)
            high, low = yhi[at], ylo[at]
            back = mm(high, inner_ref[2]) + mm(low, inner_ref[2]) + mm(high, inner_ref[3])
            for c in range(group):
                real, imag = back[c * coarse:(c + 1) * coarse, :LANES], back[c * coarse:(c + 1) * coarse, LANES:]
                lanes = slice((t * group + c) * LANES, (t * group + c + 1) * LANES)
                ehi[:coarse, lanes], elo[:coarse, lanes] = split(real * cosine - imag * sine)
                ehi[coarse:, lanes], elo[coarse:, lanes] = split(imag * cosine + real * sine)

        for t in range(per // group):
            lanes = slice(group * t * LANES, group * (t + 1) * LANES)
            high, low = ehi[:, lanes], elo[:, lanes]
            result = mm(last_ref[0], high) + mm(last_ref[0], low) + mm(last_ref[1], high)
            for c in range(group):
                for g in range(groups):
                    ybuf[pl.ds(g * per + t * group + c, seq_count, stride=4 * per)] = (
                        result[g * seq_count:(g + 1) * seq_count, c * LANES:(c + 1) * LANES])

        ysend[n] = ybuf[...].astype(BF16).reshape(seq_count, 4 * per, LANES)

        @pl.loop(0, seq_count - 1)
        def _(j):
            to = partner(j)
            back_copy(n, to, me, to).start()
        yrecv[n, me] = ysend[n, me]

    def gate(n):
        all_back(n).wait_recv()

        cut = slice(n * width, (n + 1) * width)
        ybuf[...] = yrecv[n].astype(F32).reshape(seq_count * 4 * per, LANES)
        arrived = [ybuf[pl.ds(row, seq_count, stride=4 * per)] for row in range(4 * per)]
        turned = mm_nt(eye(LANES), jnp.concatenate(arrived, axis=0).astype(BF16))
        lanes = pl.ds(pl.multiple_of(n * y_count * width + y * width, width), width)
        for g in range(groups):
            at = slice(g * LANES, (g + 1) * LANES)
            product = k_ref[at, cut].astype(F32) * v_ref[at, cut].astype(F32)
            conv = turned[:, g * width:(g + 1) * width]
            gated = q_ref[at, cut].astype(F32) * (conv + skip_ref[:, cut] * product)
            gall[at, lanes] = gated.astype(BF16)

    def send_gated(n, part):
        lanes = pl.ds(pl.multiple_of(n * y_count * width + y * width, width), width)

        @pl.loop(1, y_count)
        def _(j):
            gated_copy(n, part, lanes, y_peer(j)).start()

    def wait_gated(n, part):
        all_gated(n, part).wait_recv()

    tile = min(cols, 512)
    tiles = cols // tile

    depth = y_count * width

    def term(first, last, at, lanes):
        left = gall[at, first * depth:last * depth]
        return mm(left, wall[first:last, :, :, lanes].reshape((last - first) * depth, tile))

    def tile_at(side, step):
        return pl.ds(pl.multiple_of(side * cols + step * tile, tile), tile)

    def rows_of(part, size):
        return slice(part * size, (part + 1) * size)

    def project_ahead():
        for n in range(2):
            for part in range(2):
                wait_gated(n, part)

        @pl.loop(0, tiles)
        def _(step):
            acc[:, tile_at(0, step)] = term(0, 2, slice(0, half), tile_at(1, step))

    def project_other(part):
        at = rows_of(part, part_rows)
        for n in range(2 if part < 2 else 0, CHUNKS):
            wait_gated(n, part)

        @pl.loop(0, tiles)
        def _(step):
            if part < 2:
                total = acc[at, tile_at(0, step)] + term(2, CHUNKS, at, tile_at(1, step))
            else:
                total = term(0, CHUNKS, at, tile_at(1, step))
            psend[at, tile_at(0, step)] = total.astype(BF16)

        partial_copy(part).start()

    def project_own():
        own_copy(0).wait()
        all_pass(5).wait_recv()
        all_pass(6).wait_recv()
        for part in range(2):
            at = rows_of(part, half)

            @pl.loop(0, tiles)
            def _(step):
                own_ref[at, tile_at(0, step)] = term(0, CHUNKS, at, tile_at(0, step))

    start_blocks(0)
    prepare(1)
    start_blocks(1)
    start_w(0)
    start_w(1)
    start_w(2)
    own_copy(1).start()
    own_copy(0).start()
    for n in range(2, CHUNKS):
        prepare(n)
    for load in loads[3:]:
        load.wait()
    convolve(0)
    convolve(1)
    all_w(0).wait_recv()
    start_pass(0)
    convolve(2)
    gate(0)
    for part in range(PARTS):
        send_gated(0, part)
    convolve(3)
    all_w(1).wait_recv()
    all_pass(0).wait_recv()
    start_pass(4)
    gate(1)
    for part in range(2):
        send_gated(1, part)
    gate(2)
    for part in range(2):
        send_gated(2, part)
    own_copy(1).wait()
    all_pass(4).wait_recv()
    project_ahead()
    gate(3)
    send_gated(3, 0)
    send_gated(3, 1)
    start_w(3)
    all_w(2).wait_recv()
    start_pass(1)
    start_pass(7)
    for part in range(2, PARTS):
        for n in range(1, CHUNKS):
            send_gated(n, part)
    project_other(0)
    project_other(1)
    all_pass(1).wait_recv()
    all_pass(7).wait_recv()
    start_pass(5)
    all_w(3).wait_recv()
    start_pass(2)
    start_pass(3)
    project_other(2)
    all_pass(2).wait_recv()
    all_pass(3).wait_recv()
    start_pass(6)
    project_other(3)
    project_own()
    for part in range(PARTS):
        partial_copy(part).wait_recv()

    for n in range(CHUNKS):
        all_blocks(n).wait_send()
        all_back(n).wait_send()

    for n in range(CHUNKS):
        for part in range(PARTS):
            all_gated(n, part).wait_send()
    for kind in range(4):
        all_w(kind).wait_send()
    for route in range(8):
        all_pass(route).wait_send()
    for part in range(PARTS):
        partial_copy(part).wait_send()


def on_device(seq_count, chan_count, query_rows, key_rows, value_rows, filter_taps, skip_gain, w_out):
    rows, channels = query_rows.shape
    cols = w_out.shape[1] // chan_count
    width = channels // CHUNKS
    per = width // seq_count
    y_count = chan_count // 2
    coarse = seq_count * rows // LANES
    tables = [jnp.asarray(t) for t in transform_tables(seq_count, rows // LANES)]
    anywhere = pl.BlockSpec(memory_space=pl.ANY)
    dma = pltpu.SemaphoreType.DMA
    operands = (query_rows, key_rows, value_rows, filter_taps, skip_gain.reshape(1, channels))
    own, other = pl.pallas_call(
        functools.partial(kernel, seq_count, chan_count),
        out_shape=(pltpu.VMEM((rows, cols), F32), pltpu.VMEM((rows, cols), BF16)),
        in_specs=[anywhere] * 10,
        out_specs=(pl.BlockSpec(memory_space=pltpu.VMEM),) * 2,
        scratch_shapes=[
            *(pltpu.VMEM(x.shape, x.dtype) for x in (*operands, *tables)),
            dma((9,)),
            pltpu.VMEM((CHUNKS, seq_count, 4 * per, rows // 2), BF16),
            pltpu.VMEM((CHUNKS, seq_count, 4 * per, rows // 2), BF16),
            pltpu.VMEM((2, seq_count * 4 * per, LANES), F32),
            *(pltpu.VMEM((2 * per * coarse, 2 * LANES), BF16) for _ in range(2)),
            *(pltpu.VMEM((per * coarse, 2 * LANES), BF16) for _ in range(2)),
            *(pltpu.VMEM((2 * coarse, per * LANES), BF16) for _ in range(2)),
            pltpu.VMEM((CHUNKS, seq_count, 4 * per, LANES), BF16),
            pltpu.VMEM((CHUNKS, seq_count, 4 * per, LANES), BF16),
            pltpu.VMEM((seq_count * 4 * per, LANES), F32),
            pltpu.VMEM((rows, CHUNKS * y_count * width), BF16),
            pltpu.VMEM((CHUNKS, y_count, width, 2 * cols), BF16),
            pltpu.VMEM((rows // 2, cols), F32),
            pltpu.VMEM((rows, cols), BF16),
            dma((CHUNKS,)), dma((CHUNKS,)), dma((CHUNKS,)), dma((CHUNKS,)),
            dma((CHUNKS, PARTS)), dma((CHUNKS, PARTS)), dma((PARTS,)), dma((PARTS,)),
            dma((4,)), dma((4,)), dma((8,)), dma((8,)), dma((2,)),
        ],
        compiler_params=pltpu.CompilerParams(
            collective_id=0, has_side_effects=True, vmem_limit_bytes=56 * 1024 * 1024),
    )(*operands, w_out.reshape(CHUNKS, width, w_out.shape[1]), *tables)
    return (own + other.astype(F32)).astype(BF16)


def solution(mesh):
    return jax.shard_map(
        functools.partial(on_device, mesh.shape["seq"], mesh.shape["chan"]),
        mesh=mesh,
        in_specs=(
            P("seq", "chan"),
            P("seq", "chan"),
            P("seq", "chan"),
            P("seq", "chan"),
            P("chan"),
            P("chan", None),
        ),
        out_specs=P("seq", "chan"),
        check_vma=False,
    )
```

```python
import functools

import jax
import jax.numpy as jnp
import ml_dtypes
import numpy as np
from jax import lax
from jax.experimental import pallas as pl
from jax.experimental.pallas import tpu as pltpu
from jax.sharding import PartitionSpec as P

MESH = pl.DeviceIdType.MESH
LANES = 128
CHUNKS = 4
PARTS = 4
BF16 = jnp.bfloat16
F32 = jnp.float32


def split_table(table):
    high = table.astype(ml_dtypes.bfloat16)
    low = (table - high.astype(np.float64)).astype(ml_dtypes.bfloat16)
    return high, low


def transform_tables(seq_count, row_groups):
    coarse = seq_count * row_groups
    total = coarse * LANES
    freq = np.arange(coarse) + 0.25
    order = (np.arange(seq_count)[None, :] * row_groups + np.arange(row_groups)[:, None]).reshape(-1)
    angle = 2.0 * np.pi * freq[:, None] * order[None, :] / coarse
    forward_first = np.concatenate((np.cos(angle), -np.sin(angle)), axis=0)
    inverse_first = np.concatenate((np.cos(angle).T, -np.sin(angle).T), axis=1) / total
    fine = np.arange(LANES)
    turn = 2.0 * np.pi * freq[:, None] * fine[None, :] / total
    twist_cos = np.cos(turn).astype(np.float32)
    twist_sin = np.sin(turn).astype(np.float32)
    inner = 2.0 * np.pi * (fine[:, None] * fine[None, :] % LANES) / LANES
    cosine, sine = np.cos(inner), np.sin(inner)
    forward_second = np.block([[cosine, -sine], [sine, cosine]])
    inverse_second = np.block([[cosine, sine], [-sine, cosine]])
    turns = np.stack((twist_cos, twist_sin))
    inner = np.stack((*split_table(forward_second), *split_table(inverse_second)))
    first = np.concatenate(split_table(forward_first), axis=1)
    last = np.stack(split_table(inverse_first))
    return turns, inner, first, last


def mm(left, right):
    return jnp.dot(left, right, preferred_element_type=F32)


def mm_nt(left, right):
    return lax.dot_general(left, right, (((1,), (1,)), ((), ())), preferred_element_type=F32)


def split(value):
    high = value.astype(BF16)
    low = (value - high.astype(F32)).astype(BF16)
    return high, low


def eye(size):
    row = lax.broadcasted_iota(jnp.int32, (size, size), 0)
    col = lax.broadcasted_iota(jnp.int32, (size, size), 1)
    return (row == col).astype(F32).astype(BF16)


def by_owner(seq_count, per):
    width = seq_count * per
    row = lax.broadcasted_iota(jnp.int32, (2 * width, 2 * width), 0)
    col = lax.broadcasted_iota(jnp.int32, (2 * width, 2 * width), 1)
    picked = row // per % 2 * width + row % per * seq_count + row // (2 * per)
    return (picked == col).astype(F32).astype(BF16)


def kernel(
    seq_count, chan_count,
    q_hbm, k_hbm, v_hbm, h_hbm, skip_hbm, w_ref, turns_hbm, inner_hbm, first_hbm, last_hbm,
    own_ref, precv,
    q_ref, k_ref, v_ref, h_ref, skip_ref, turns_ref, inner_ref, first_ref, last_ref, load_sem,
    send, recv, staged, zhi, zlo, yhi, ylo, ehi, elo, ysend, yrecv, ybuf, gall, wall, acc, psend,
    send_sem, recv_sem, ysend_sem, yrecv_sem, gsend_sem, grecv_sem, psend_sem, precv_sem,
    wsend_sem, wrecv_sem, fsend_sem, frecv_sem, wown_sem,
):
    rows, channels = q_ref.shape
    groups = rows // LANES
    width = channels // CHUNKS
    per = width // seq_count
    coarse = seq_count * groups
    cols = own_ref.shape[1]
    y_count = chan_count // 2
    half = rows // 2
    levels = seq_count // 4
    part_rows = rows // PARTS
    me = lax.axis_index("seq")
    chan = lax.axis_index("chan")
    core = me % 2
    x_lo = (me // 2) % 2
    parity = (me // 4) % 2
    above = (me + 4) % seq_count
    below = (me + seq_count - 4) % seq_count
    sibling = me + 1 - 2 * core
    mate = me + 2 - 4 * x_lo
    x_hi = chan // y_count
    y = chan % y_count
    facing = (1 - x_hi) * y_count + y

    def y_peer(j):
        return (y + j) % y_count

    def partner(j):
        group = (j + j // (seq_count - 4)) // 4
        shift = (group // 2 + 1) * (1 - 2 * (group % 2)) * (1 - group // (levels - 1))
        turn = (j + j // (seq_count - 4)) % 4
        return (me // 4 + shift + levels) % levels * 4 + (me % 4 + turn) % 4

    def device(seq_to, chan_to):
        return {"seq": seq_to, "chan": chan_to}

    barrier = pltpu.get_barrier_semaphore()

    @pl.loop(1, seq_count)
    def _(j):
        pl.semaphore_signal(barrier, inc=1, device_id=device((me + j) % seq_count, chan), device_id_type=MESH)

    @pl.loop(1, y_count)
    def _(j):
        pl.semaphore_signal(barrier, inc=1, device_id=device(me, x_hi * y_count + y_peer(j)), device_id_type=MESH)

    pl.semaphore_signal(barrier, inc=1, device_id=device(me, facing), device_id_type=MESH)

    loads = [pltpu.make_async_copy(source, target, load_sem.at[i]) for i, (source, target) in enumerate((
        (k_hbm, k_ref), (v_hbm, v_ref), (h_hbm, h_ref), (turns_hbm, turns_ref), (inner_hbm, inner_ref),
        (first_hbm, first_ref), (last_hbm, last_ref), (q_hbm, q_ref), (skip_hbm, skip_ref)))]
    for load in loads:
        load.start()
    for load in loads[:3]:
        load.wait()

    def prepare(n):
        cut = slice(n * width, (n + 1) * width)
        product = (k_ref[:, cut].astype(F32) * v_ref[:, cut].astype(F32)).astype(BF16)
        both = jnp.concatenate((product, h_ref[:, cut].astype(BF16)), axis=1)
        ordered = mm_nt(by_owner(seq_count, per), both).reshape(seq_count, 2 * per, rows)
        send[n] = jnp.concatenate((ordered[:, :, :half], ordered[:, :, half:]), axis=1).astype(BF16)

    prepare(0)
    pl.semaphore_wait(barrier, seq_count + y_count - 1)

    def block_copy(n, slot_out, slot_in, to):
        return pltpu.make_async_remote_copy(
            src_ref=send.at[n, slot_out], dst_ref=recv.at[n, slot_in],
            send_sem=send_sem.at[n], recv_sem=recv_sem.at[n],
            device_id={"seq": to, "chan": chan}, device_id_type=MESH)

    def back_copy(n, slot_out, slot_in, to):
        return pltpu.make_async_remote_copy(
            src_ref=ysend.at[n, slot_out], dst_ref=yrecv.at[n, slot_in],
            send_sem=ysend_sem.at[n], recv_sem=yrecv_sem.at[n],
            device_id={"seq": to, "chan": chan}, device_id_type=MESH)

    def gated_copy(n, part, lanes, to):
        block = gall.at[pl.ds(part * part_rows, part_rows), lanes]
        return pltpu.make_async_remote_copy(
            src_ref=block, dst_ref=block,
            send_sem=gsend_sem.at[n, part], recv_sem=grecv_sem.at[n, part],
            device_id=device(me, x_hi * y_count + to), device_id_type=MESH)

    def all_gated(n, part):
        return gated_copy(n, part, pl.ds(0, (y_count - 1) * width), y)

    def partial_copy(part):
        at = pl.ds(part * part_rows, part_rows)
        return pltpu.make_async_remote_copy(
            src_ref=psend.at[at], dst_ref=precv.at[at],
            send_sem=psend_sem.at[part], recv_sem=precv_sem.at[part],
            device_id=device(me, facing), device_id_type=MESH)

    core_rows = width // 2
    by_pair = width // 8
    first_half, last_half = pl.ds(0, CHUNKS // 2), pl.ds(CHUNKS // 2, CHUNKS // 2)
    w_chunks = (pl.ds(0, CHUNKS), pl.ds(0, CHUNKS), first_half, last_half)
    w_rows = (by_pair, core_rows - 2 * by_pair, core_rows // 2, core_rows // 2)
    w_side = (1, 1, 0, 0)

    def w_start(kind):
        return core * core_rows + (x_lo * by_pair, 2 * by_pair, parity * (core_rows // 2), parity * (core_rows // 2))[kind]

    def some_rows(start, size):
        return pl.ds(pl.multiple_of(start, 16), size)

    def lanes_of(side):
        return pl.ds(side * cols, cols)

    def side_of(col_side, x_side, y_side):
        target = jnp.where(col_side == 0, x_side, 1 - x_side)
        return pl.ds(pl.multiple_of((target * y_count + y_side) * cols, cols), cols)

    def w_copy(kind, to):
        at, side = some_rows(w_start(kind), w_rows[kind]), w_side[kind]
        return pltpu.make_async_remote_copy(
            src_ref=w_ref.at[w_chunks[kind], at, side_of(side, x_hi, to)], dst_ref=wall.at[w_chunks[kind], y, at, lanes_of(side)],
            send_sem=wsend_sem.at[kind], recv_sem=wrecv_sem.at[kind],
            device_id=device(me, x_hi * y_count + to), device_id_type=MESH)

    def all_w(kind):
        block = wall.at[w_chunks[kind], pl.ds(0, y_count - 1), pl.ds(0, w_rows[kind]), lanes_of(0)]
        return pltpu.make_async_remote_copy(
            src_ref=block, dst_ref=block, send_sem=wsend_sem.at[kind], recv_sem=wrecv_sem.at[kind],
            device_id=device(me, facing), device_id_type=MESH)

    quarter = core_rows // 4
    pass_rows = (by_pair, quarter, quarter, quarter, core_rows, core_rows, core_rows, quarter)
    pass_side = (1, 0, 0, 0, 1, 0, 0, 0)
    every = pl.ds(0, CHUNKS)
    pass_chunks = (every, first_half, last_half, last_half, every, first_half, last_half, first_half)
    pass_to = (mate, above, above, below, sibling, sibling, sibling, below)

    def w_pass(route, slot):
        up, down = parity * 2 * quarter, (parity * 2 + 1) * quarter
        start = core * core_rows + (x_lo * by_pair, up, up, down, 0, 0, 0, down)[route]
        block = wall.at[pass_chunks[route], slot, some_rows(start, pass_rows[route]), lanes_of(pass_side[route])]
        return pltpu.make_async_remote_copy(
            src_ref=block, dst_ref=block, send_sem=fsend_sem.at[route], recv_sem=frecv_sem.at[route],
            device_id=device(pass_to[route], chan), device_id_type=MESH)

    def all_pass(route):
        block = wall.at[pass_chunks[route], pl.ds(0, y_count - 1), pl.ds(0, pass_rows[route]), lanes_of(0)]
        return pltpu.make_async_remote_copy(
            src_ref=block, dst_ref=block, send_sem=fsend_sem.at[route], recv_sem=frecv_sem.at[route],
            device_id=device(pass_to[route], chan), device_id_type=MESH)

    def own_copy(col_side):
        return pltpu.make_async_copy(
            w_ref.at[:, :, side_of(col_side, x_hi, y)],
            wall.at[:, y, :, pl.ds(col_side * cols, cols)], wown_sem.at[col_side])

    def start_w(kind):
        @pl.loop(1, y_count)
        def _(j):
            w_copy(kind, y_peer(j)).start()

    def start_pass(route):
        @pl.loop(1, y_count)
        def _(j):
            w_pass(route, y_peer(j)).start()

    def start_blocks(n):
        @pl.loop(0, seq_count - 1)
        def _(j):
            to = partner(j)
            block_copy(n, to, me, to).start()
        recv[n, me] = send[n, me]

    others = pl.ds(0, seq_count - 1)

    def all_blocks(n):
        return block_copy(n, others, others, me)

    def all_back(n):
        return back_copy(n, others, others, me)

    def convolve(n):
        all_blocks(n).wait_recv()
        if n + 2 < CHUNKS:
            start_blocks(n + 2)

        for g in range(2):
            staged[g] = recv[n, :, :, g * LANES:(g + 1) * LANES].astype(F32).reshape(seq_count * 4 * per, LANES)

        def gather_rows(row):
            parts = [staged[g % 2, pl.ds(g // 2 * 2 * per + row, seq_count, stride=4 * per)] for g in range(groups)]
            return jnp.concatenate(parts, axis=0)

        cosine, sine = turns_ref[0], turns_ref[1]
        cosines, sines = jnp.concatenate((cosine, cosine), axis=1), jnp.concatenate((sine, sine), axis=1)
        for c in range(per):
            signal = jnp.concatenate((gather_rows(c), gather_rows(c + per)), axis=1).astype(BF16)
            stage = mm(first_ref[...], jnp.concatenate((signal, signal), axis=0))
            real, imag = stage[:coarse], stage[coarse:]
            turned_re = real * cosines + imag * sines
            turned_im = imag * cosines - real * sines
            for side in range(2):
                at = slice((2 * c + side) * coarse, (2 * c + side + 1) * coarse)
                lanes = slice(side * LANES, (side + 1) * LANES)
                zhi[at, :LANES], zlo[at, :LANES] = split(turned_re[:, lanes])
                zhi[at, LANES:], zlo[at, LANES:] = split(turned_im[:, lanes])

        group = min(per, 4)
        for t in range(per // group):
            at = slice(2 * group * t * coarse, 2 * group * (t + 1) * coarse)
            high, low = zhi[at], zlo[at]
            both = mm(high, inner_ref[0]) + mm(low, inner_ref[0]) + mm(high, inner_ref[1])
            for c in range(group):
                p_re, p_im = both[2 * c * coarse:(2 * c + 1) * coarse, :LANES], both[2 * c * coarse:(2 * c + 1) * coarse, LANES:]
                h_re, h_im = both[(2 * c + 1) * coarse:(2 * c + 2) * coarse, :LANES], both[(2 * c + 1) * coarse:(2 * c + 2) * coarse, LANES:]
                at = slice((t * group + c) * coarse, (t * group + c + 1) * coarse)
                yhi[at, :LANES], ylo[at, :LANES] = split(p_re * h_re - p_im * h_im)
                yhi[at, LANES:], ylo[at, LANES:] = split(p_re * h_im + p_im * h_re)

        for t in range(per // group):
            at = slice(group * t * coarse, group * (t + 1) * coarse)
            high, low = yhi[at], ylo[at]
            back = mm(high, inner_ref[2]) + mm(low, inner_ref[2]) + mm(high, inner_ref[3])
            for c in range(group):
                real, imag = back[c * coarse:(c + 1) * coarse, :LANES], back[c * coarse:(c + 1) * coarse, LANES:]
                lanes = slice((t * group + c) * LANES, (t * group + c + 1) * LANES)
                ehi[:coarse, lanes], elo[:coarse, lanes] = split(real * cosine - imag * sine)
                ehi[coarse:, lanes], elo[coarse:, lanes] = split(imag * cosine + real * sine)

        for t in range(per // group):
            lanes = slice(group * t * LANES, group * (t + 1) * LANES)
            high, low = ehi[:, lanes], elo[:, lanes]
            result = mm(last_ref[0], high) + mm(last_ref[0], low) + mm(last_ref[1], high)
            for c in range(group):
                for g in range(groups):
                    ybuf[pl.ds(g * per + t * group + c, seq_count, stride=4 * per)] = (
                        result[g * seq_count:(g + 1) * seq_count, c * LANES:(c + 1) * LANES])

        ysend[n] = ybuf[...].astype(BF16).reshape(seq_count, 4 * per, LANES)

        @pl.loop(0, seq_count - 1)
        def _(j):
            to = partner(j)
            back_copy(n, to, me, to).start()
        yrecv[n, me] = ysend[n, me]

    def gate(n):
        all_back(n).wait_recv()

        cut = slice(n * width, (n + 1) * width)
        ybuf[...] = yrecv[n].astype(F32).reshape(seq_count * 4 * per, LANES)
        arrived = [ybuf[pl.ds(row, seq_count, stride=4 * per)] for row in range(4 * per)]
        turned = mm_nt(eye(LANES), jnp.concatenate(arrived, axis=0).astype(BF16))
        lanes = pl.ds(pl.multiple_of(n * y_count * width + y * width, width), width)
        for g in range(groups):
            at = slice(g * LANES, (g + 1) * LANES)
            product = k_ref[at, cut].astype(F32) * v_ref[at, cut].astype(F32)
            conv = turned[:, g * width:(g + 1) * width]
            gated = q_ref[at, cut].astype(F32) * (conv + skip_ref[:, cut] * product)
            gall[at, lanes] = gated.astype(BF16)

    def send_gated(n, part):
        lanes = pl.ds(pl.multiple_of(n * y_count * width + y * width, width), width)

        @pl.loop(1, y_count)
        def _(j):
            gated_copy(n, part, lanes, y_peer(j)).start()

    def wait_gated(n, part):
        all_gated(n, part).wait_recv()

    tile = min(cols, 512)
    tiles = cols // tile

    depth = y_count * width

    def term(first, last, at, lanes):
        left = gall[at, first * depth:last * depth]
        return mm(left, wall[first:last, :, :, lanes].reshape((last - first) * depth, tile))

    def tile_at(side, step):
        return pl.ds(pl.multiple_of(side * cols + step * tile, tile), tile)

    def rows_of(part, size):
        return slice(part * size, (part + 1) * size)

    def project_ahead():
        for n in range(2):
            for part in range(2):
                wait_gated(n, part)

        @pl.loop(0, tiles)
        def _(step):
            acc[:, tile_at(0, step)] = term(0, 2, slice(0, half), tile_at(1, step))

    def project_other(part):
        at = rows_of(part, part_rows)
        for n in range(2 if part < 2 else 0, CHUNKS):
            wait_gated(n, part)

        @pl.loop(0, tiles)
        def _(step):
            if part < 2:
                total = acc[at, tile_at(0, step)] + term(2, CHUNKS, at, tile_at(1, step))
            else:
                total = term(0, CHUNKS, at, tile_at(1, step))
            psend[at, tile_at(0, step)] = total.astype(BF16)

        partial_copy(part).start()

    def project_own():
        own_copy(0).wait()
        all_pass(5).wait_recv()
        all_pass(6).wait_recv()
        for part in range(2):
            at = rows_of(part, half)

            @pl.loop(0, tiles)
            def _(step):
                own_ref[at, tile_at(0, step)] = term(0, CHUNKS, at, tile_at(0, step))

    start_blocks(0)
    prepare(1)
    start_blocks(1)
    start_w(0)
    start_w(1)
    start_w(2)
    own_copy(1).start()
    own_copy(0).start()
    for n in range(2, CHUNKS):
        prepare(n)
    for load in loads[3:]:
        load.wait()
    convolve(0)
    convolve(1)
    all_w(0).wait_recv()
    start_pass(0)
    convolve(2)
    gate(0)
    for part in range(PARTS):
        send_gated(0, part)
    convolve(3)
    gate(1)
    for part in range(2):
        send_gated(1, part)
    all_w(1).wait_recv()
    all_pass(0).wait_recv()
    start_pass(4)
    gate(2)
    for part in range(2):
        send_gated(2, part)
    own_copy(1).wait()
    all_pass(4).wait_recv()
    project_ahead()
    gate(3)
    send_gated(3, 0)
    send_gated(3, 1)
    start_w(3)
    all_w(2).wait_recv()
    start_pass(1)
    start_pass(7)
    for part in range(2, PARTS):
        for n in range(1, CHUNKS):
            send_gated(n, part)
    project_other(0)
    project_other(1)
    all_pass(1).wait_recv()
    all_pass(7).wait_recv()
    start_pass(5)
    all_w(3).wait_recv()
    start_pass(2)
    start_pass(3)
    project_other(2)
    all_pass(2).wait_recv()
    all_pass(3).wait_recv()
    start_pass(6)
    project_other(3)
    project_own()
    for part in range(PARTS):
        partial_copy(part).wait_recv()

    for n in range(CHUNKS):
        all_blocks(n).wait_send()
        all_back(n).wait_send()

    for n in range(CHUNKS):
        for part in range(PARTS):
            all_gated(n, part).wait_send()
    for kind in range(4):
        all_w(kind).wait_send()
    for route in range(8):
        all_pass(route).wait_send()
    for part in range(PARTS):
        partial_copy(part).wait_send()


def on_device(seq_count, chan_count, query_rows, key_rows, value_rows, filter_taps, skip_gain, w_out):
    rows, channels = query_rows.shape
    cols = w_out.shape[1] // chan_count
    width = channels // CHUNKS
    per = width // seq_count
    y_count = chan_count // 2
    coarse = seq_count * rows // LANES
    tables = [jnp.asarray(t) for t in transform_tables(seq_count, rows // LANES)]
    anywhere = pl.BlockSpec(memory_space=pl.ANY)
    dma = pltpu.SemaphoreType.DMA
    operands = (query_rows, key_rows, value_rows, filter_taps, skip_gain.reshape(1, channels))
    own, other = pl.pallas_call(
        functools.partial(kernel, seq_count, chan_count),
        out_shape=(pltpu.VMEM((rows, cols), F32), pltpu.VMEM((rows, cols), BF16)),
        in_specs=[anywhere] * 10,
        out_specs=(pl.BlockSpec(memory_space=pltpu.VMEM),) * 2,
        scratch_shapes=[
            *(pltpu.VMEM(x.shape, x.dtype) for x in (*operands, *tables)),
            dma((9,)),
            pltpu.VMEM((CHUNKS, seq_count, 4 * per, rows // 2), BF16),
            pltpu.VMEM((CHUNKS, seq_count, 4 * per, rows // 2), BF16),
            pltpu.VMEM((2, seq_count * 4 * per, LANES), F32),
            *(pltpu.VMEM((2 * per * coarse, 2 * LANES), BF16) for _ in range(2)),
            *(pltpu.VMEM((per * coarse, 2 * LANES), BF16) for _ in range(2)),
            *(pltpu.VMEM((2 * coarse, per * LANES), BF16) for _ in range(2)),
            pltpu.VMEM((CHUNKS, seq_count, 4 * per, LANES), BF16),
            pltpu.VMEM((CHUNKS, seq_count, 4 * per, LANES), BF16),
            pltpu.VMEM((seq_count * 4 * per, LANES), F32),
            pltpu.VMEM((rows, CHUNKS * y_count * width), BF16),
            pltpu.VMEM((CHUNKS, y_count, width, 2 * cols), BF16),
            pltpu.VMEM((rows // 2, cols), F32),
            pltpu.VMEM((rows, cols), BF16),
            dma((CHUNKS,)), dma((CHUNKS,)), dma((CHUNKS,)), dma((CHUNKS,)),
            dma((CHUNKS, PARTS)), dma((CHUNKS, PARTS)), dma((PARTS,)), dma((PARTS,)),
            dma((4,)), dma((4,)), dma((8,)), dma((8,)), dma((2,)),
        ],
        compiler_params=pltpu.CompilerParams(
            collective_id=0, has_side_effects=True, vmem_limit_bytes=56 * 1024 * 1024),
    )(*operands, w_out.reshape(CHUNKS, width, w_out.shape[1]), *tables)
    return (own + other.astype(F32)).astype(BF16)


def solution(mesh):
    return jax.shard_map(
        functools.partial(on_device, mesh.shape["seq"], mesh.shape["chan"]),
        mesh=mesh,
        in_specs=(
            P("seq", "chan"),
            P("seq", "chan"),
            P("seq", "chan"),
            P("seq", "chan"),
            P("chan"),
            P("chan", None),
        ),
        out_specs=P("seq", "chan"),
        check_vma=False,
    )
```
